128 devices in a mesh: blk: 32 (over z, y, x_hi), img: 4 (over x_lo, core).
Axes of the slice: x: 4 (x_hi: 2, x_lo: 2; x = x_hi * 2 + x_lo), y: 4, z: 4, core: 2. Of those that a mesh axis runs over, the one named last changes fastest.
Arguments:
- images: bfloat16 [16384, 1152], P(('blk', 'img')), may hold values from -0.1875 to 0.1875
- texts: bfloat16 [16384, 1152], P(('blk', 'img')), may hold values from -0.1875 to 0.1875
- cache: bfloat16 [16384, 1152], P(('blk', 'img')), may hold values from -0.1875 to 0.1875
- mate_owner: int32 [16384, 4], P(('blk', 'img')), may hold values from 0 to 127, all different within a row; in each aligned block of 128 rows (0 to 127, 128 to 255, ...) at most 8 rows name the same one
- mate_row: int32 [16384, 4], P(('blk', 'img')), may hold values from 0 to 127
- mate_count: int32 [16384], P(('blk', 'img')), may hold values from 1 to 4
- log_scale: float32 [1], replicated, may hold values from 1.8 to 2.6
- bias: float32 [1], replicated, may hold values from -6 to -2
Outputs:
- image_grad: float32 [16384, 1152], P(('blk', 'img'))
- text_grad: float32 [16384, 1152], P(('blk', 'img'))
- cache_grad: float32 [16384, 1152], P(('blk', 'img'))
The draws below stay inside these ranges and needn't reach their ends.
Inputs may be any that keep to these rules, and one draw needn't show every extreme that they name: `mate_owner`: among the 4 entries of the 128 rows of one device, each owner is named at most 8 times, and some device names some owner exactly 8 times; within a row the owners differ.
All inputs are finite; a program needn't handle non-finite values.
Results may differ from the reference program's by a relative error of at most 0.0034.
Values may be sent and summed in bfloat16 or wider, within the bound.
A program may use at most 128 MiB of HBM per device.

```python
import math
import jax
import jax.numpy as jnp
import numpy as np
from jax import lax

D = 1152
IMG_DEV = 128
MATES = 4
CACHE_DEV = 128
PAIRS = 16384
OWNERS = 128
CACHE_ROWS = 16384
CAP = 8


def touch_ends(values, rng, smallest, top_value):
    longest = values.shape.index(max(values.shape))
    spots = []
    for shift in (0, 1):
        where = [jax.random.randint(jax.random.fold_in(rng, axis), (), 0, length) for axis, length in enumerate(values.shape)]
        where[longest] = (where[longest] + shift) % values.shape[longest]
        spots.append(tuple(where))
    return values.at[spots[0]].set(smallest).at[spots[1]].set(top_value)


def level_of(own_key, dims, shards, low, largest):
    def one(position, blocks):
        steps = jax.random.uniform(jax.random.fold_in(jax.random.fold_in(own_key, 6), position), (blocks,), jnp.float32, low / len(shards), largest / len(shards))
        return jnp.repeat(jnp.exp(steps), dims[position] // blocks).reshape((-1,) + (1,) * (len(dims) - position - 1))

    factor_of = one(*shards[0])
    for cut in shards[1:]:
        factor_of = factor_of * one(*cut)
    return factor_of


def deal_out(key, own, number, rows, amount, top, reach, slope):
    ranking = jax.random.permutation(key, amount)
    packed, usual = shares(amount, rows * top, reach, slope, True), shares(amount, rows * top, reach, slope, False)
    places = jnp.arange(amount)

    def named(sizes, rotation):
        used = int((sizes > 0).sum())
        fixed = max(1, used // 4)
        moved = fixed + (places - fixed + rotation * (used - fixed)) % max(1, amount - fixed)
        return jnp.zeros((amount,), jnp.int32).at[ranking[jnp.where(places < fixed, places, moved)]].set(jnp.asarray(sizes, jnp.int32))

    sizes = jnp.where(number % 4 == 0, named(packed, number // 4), named(usual, number - number // 4 - 1))
    mixed = jax.random.permutation(jax.random.fold_in(own, 3), amount)
    donor, receiver = mixed[0:amount // 2 * 2:2], mixed[1:amount // 2 * 2:2]
    room = jnp.minimum(sizes[donor] - 1, reach - sizes[receiver]) // 2
    room = jnp.where((donor == ranking[0]) | (receiver == ranking[0]) | (sizes[receiver] == 0), 0, jnp.maximum(room, 0))
    moved = jax.random.randint(jax.random.fold_in(own, 4), (amount // 2,), 0, 1 << 20) % (room + 1)
    sizes = sizes.at[donor].add(-moved).at[receiver].add(moved)
    labels = jnp.searchsorted(jnp.cumsum(sizes), jnp.arange(rows * top), side="right").astype(jnp.int32)
    listing = labels.reshape(top, rows).T
    listing = listing[jax.random.permutation(jax.random.fold_in(own, 1), rows)]
    rotation = jax.random.randint(jax.random.fold_in(own, 2), (rows, 1), 0, top)
    return jnp.take_along_axis(listing, (jnp.arange(top)[None, :] + rotation) % top, axis=1)


def shares(count, total, bound, skew, full):
    portions = [(1 << 20) // math.isqrt(grade ** skew) + 1 for grade in range(1, count + 1)]
    largest = bound if full else min(bound, max(-(-total // count), total * portions[0] // sum(portions)))
    least = 1 if total - largest >= count - 1 else 0
    holding, surplus = [largest] + [least] * (count - 1), total - largest - least * (count - 1)
    while surplus > 0:
        movable = [i for i in range(1, count) if holding[i] < largest] or [i for i in range(1, count) if holding[i] < bound]
        pool, left = sum([portions[i] for i in movable]), surplus
        for i in movable:
            addition = min(bound - holding[i], max(1, left * portions[i] // pool), surplus)
            holding[i] = holding[i] + addition
            surplus = surplus - addition
    return np.array(holding)


def scatter_about(stream_key, extent, deviation, reach, split=(), kind=jnp.bfloat16):
    loudness = level_of(stream_key, extent, split, -0.22, 0.18) if split else 1.0
    values = jax.random.normal(stream_key, extent, jnp.float32) * deviation * loudness
    return jnp.minimum(jnp.maximum(values, -reach), reach).astype(kind)


def setup_inputs(seed: int = 0) -> dict:
    arg_keys = jax.random.split(jax.random.key(seed), 9)
    images = scatter_about(arg_keys[0], (PAIRS, D), 0.03, 0.1875, ((0, 128),))
    texts = scatter_about(arg_keys[1], (PAIRS, D), 0.03, 0.1875, ((0, 128),))
    cache = scatter_about(arg_keys[2], (CACHE_ROWS, D), 0.03, 0.1875, ((0, 128),))
    mate_owner_keys = jax.random.split(jax.random.fold_in(arg_keys[3], 1), PAIRS // IMG_DEV)
    mate_owner_turns = jax.random.permutation(jax.random.fold_in(arg_keys[3], 3), PAIRS // IMG_DEV)
    mate_owner = jax.vmap(lambda own, number: deal_out(jax.random.fold_in(arg_keys[3], 2), own, number, IMG_DEV, OWNERS, MATES, CAP, 2))(mate_owner_keys, mate_owner_turns).reshape((PAIRS, MATES))
    mate_row = touch_ends(jax.random.randint(arg_keys[4], (PAIRS, MATES), 0, CACHE_DEV), jax.random.fold_in(arg_keys[4], 1), 0, CACHE_DEV - 1).astype(jnp.int32)
    mate_count = touch_ends(jax.random.randint(arg_keys[5], (PAIRS,), 1, MATES + 1), jax.random.fold_in(arg_keys[5], 1), 1, MATES).astype(jnp.int32)
    log_scale = jnp.clip(jax.random.uniform(arg_keys[6], (1,), jnp.float32, 1.8, 2.6), 1.8, 2.6)
    bias = jnp.clip(jax.random.uniform(arg_keys[7], (1,), jnp.float32, -6.0, -2.0), -6.0, -2.0)
    return dict(images=images, texts=texts, cache=cache, mate_owner=mate_owner, mate_row=mate_row, mate_count=mate_count, log_scale=log_scale, bias=bias)


def reference(images, texts, cache, mate_owner, mate_row, mate_count, log_scale, bias):
    scale = jnp.exp(log_scale[0])
    offset = bias[0]
    total_rows = images.shape[0]
    width = images.shape[1]
    block = min(512, total_rows)
    count = total_rows // block
    columns = jnp.arange(total_rows, dtype=jnp.int32)

    def step(tgrad, index):
        start = (index * block).astype(jnp.int32)
        rows_img = lax.dynamic_slice_in_dim(images, start, block, 0)
        logits = scale * jnp.dot(rows_img, texts.T, preferred_element_type=jnp.float32) + offset
        ids = start + jnp.arange(block, dtype=jnp.int32)
        same = (ids[:, None] == columns[None, :]).astype(jnp.float32)
        coeff = (scale * (jax.nn.sigmoid(logits) - same)).astype(jnp.bfloat16)
        igrad = jnp.dot(coeff, texts, preferred_element_type=jnp.float32)
        tgrad = tgrad + jnp.dot(coeff.T, rows_img, preferred_element_type=jnp.float32)
        return tgrad, igrad

    text_grad, image_parts = lax.scan(step, jnp.zeros((total_rows, width), jnp.float32), jnp.arange(count, dtype=jnp.int32))
    image_grad = image_parts.reshape(total_rows, width)
    ids = (mate_owner * CACHE_DEV + mate_row).astype(jnp.int32)
    mate_emb = cache[ids]
    mate_logit = scale * jnp.einsum("rd,rkd->rk", images.astype(jnp.float32), mate_emb.astype(jnp.float32)) + offset
    live = jnp.arange(MATES, dtype=jnp.int32)[None, :] < mate_count[:, None]
    mate_coeff = jnp.where(live, scale * (jax.nn.sigmoid(mate_logit) - 1.0), 0.0).astype(jnp.bfloat16)
    image_grad = image_grad + jnp.einsum("rk,rkd->rd", mate_coeff.astype(jnp.float32), mate_emb.astype(jnp.float32))
    terms = mate_coeff.astype(jnp.float32)[:, :, None] * images.astype(jnp.float32)[:, None, :]
    cache_grad = jnp.zeros((CACHE_ROWS, width), jnp.float32).at[ids.reshape(-1)].add(terms.reshape(-1, width))
    return image_grad, text_grad, cache_grad
```

```python
import jax
import jax.numpy as jnp
from jax import lax
from jax.experimental import pallas as pl
from jax.experimental.pallas import tpu as pltpu
from jax.sharding import PartitionSpec as P

MESH = pl.DeviceIdType.MESH
F32, BF16, I32 = jnp.float32, jnp.bfloat16, jnp.int32
NT = (((1,), (1,)), ((), ()))
NN = (((1,), (0,)), ((), ()))
TN = (((0,), (0,)), ((), ()))
ROWS, D, HALF = 128, 1152, 64
LO, HI = pl.ds(0, HALF), pl.ds(HALF, HALF)


def mm(a, b, dims):
    return lax.dot_general(a, b, dims, preferred_element_type=F32)


def kernel(
    ls_ref, bias_ref, images, texts, cache, owner, row, count,
    ig_out, tg_out, cg_out,
    img, txt, cac, gat, tbl, coeff, tgrad, part, pbf, sgr,
    ra1, rb1, ra2, rb2, sa2, sb2, tsib, trec, csib, crec, tsx, trx, csx, crx,
    a_s, a_r, b_s, b_r, t_s, t_r, c_s, c_r, k_s, k_r,
    ra1_s, ra1_r, rb1_s, rb1_r, r2_s, r2_r, x_s, x_r,
):
    blk, im = lax.axis_index("blk"), lax.axis_index("img")
    z, y, x, c = blk // 8, (blk // 2) % 4, (blk % 2) * 2 + im // 2, im % 2

    def dev(dz=0, dy=0, dx=0, dc=0):
        zz, yy, xx = (z + dz + 4) % 4, (y + dy + 4) % 4, (x + dx + 4) % 4
        return ((zz * 4 + yy) * 2 + xx // 2, (xx % 2) * 2 + (c + dc) % 2)

    def rc(src, dst, ss, rs, to):
        return pltpu.make_async_remote_copy(
            src_ref=src, dst_ref=dst, send_sem=ss, recv_sem=rs, device_id=to, device_id_type=MESH
        )

    def img_a(dz, dy, d_z, d_y):
        return rc(img.at[dz * 4 + dy, LO], img.at[(dz + d_z) * 4 + dy + d_y, LO],
                  a_s.at[dz + d_z, dy + d_y], a_r.at[dz + d_z, dy + d_y], dev(-d_z, -d_y))

    def img_b(dz, dy, d_z, d_y):
        return rc(img.at[dz * 4 + dy, HI], img.at[(dz + d_z) * 4 + dy + d_y, HI],
                  b_s.at[dz + d_z, dy + d_y], b_r.at[dz + d_z, dy + d_y], dev(-d_z, -d_y))

    def got_a(dz, dy):
        rc(img.at[dz * 4 + dy, LO], img.at[dz * 4 + dy, LO], a_s.at[dz, dy], a_r.at[dz, dy], dev(0, 1)).wait_recv()

    def got_b(dz, dy):
        rc(img.at[dz * 4 + dy, HI], img.at[dz * 4 + dy, HI], b_s.at[dz, dy], b_r.at[dz, dy], dev(0, 1)).wait_recv()

    def rows_of(ref, n):
        return ref.at[pl.ds(n * ROWS, ROWS)]

    def along_x(ref, sems, semr, d):
        return rc(rows_of(ref, 0), rows_of(ref, 2 * d), sems.at[2 * d], semr.at[2 * d], dev(dx=-d))

    def to_sib(ref, sems, semr, d):
        return rc(rows_of(ref, 2 * d), rows_of(ref, 2 * d + 1), sems.at[2 * d + 1], semr.at[2 * d + 1], dev(dc=1))

    def tbl_y(d):
        return rc(tbl.at[0, 0], tbl.at[0, d], k_s.at[d], k_r.at[d], dev(0, -d))

    def tbl_z(d):
        return rc(tbl.at[0], tbl.at[d], k_s.at[3 + d], k_r.at[3 + d], dev(-d))

    peers = [dev(dy=d) for d in (1, 2, 3)] + [dev(dz=d) for d in (1, 2, 3)]
    peers += [dev(dx=d) for d in (1, 2, 3)] + [dev(dc=1)]
    barrier = pltpu.get_barrier_semaphore()
    for to in peers:
        pl.semaphore_signal(barrier, inc=1, device_id=to, device_id_type=MESH)
    img[0] = images[...]
    txt[0:ROWS] = texts[...]
    cac[0:ROWS] = cache[...]
    pl.semaphore_wait(barrier, len(peers))

    for d in (1, 3, 2):
        along_x(txt, t_s, t_r, d).start()
        img_a(0, 0, 0, d).start()
        img_b(0, 0, d, 0).start()
    to_sib(txt, t_s, t_r, 0).start()
    for d in (1, 3, 2):
        img_a(0, 0, d, 0).start()
        img_b(0, 0, 0, d).start()

    lane = lax.broadcasted_iota(I32, (ROWS, ROWS), 1)
    sub = lax.broadcasted_iota(I32, (ROWS, ROWS), 0)
    below = (sub > lane).astype(BF16)
    live = jnp.sum(jnp.where(sub == lane, count[...].astype(F32), 0.0), axis=1, keepdims=True)
    carry = jnp.zeros((1, ROWS), F32)
    picked_r = [jnp.zeros((1, ROWS), F32) for _ in range(8)]
    picked_c = [jnp.zeros((1, ROWS), F32) for _ in range(8)]
    row1 = (sub + 1).astype(F32)
    for k in range(4):
        hits = ((owner[:, k : k + 1] == lane) & (live > k)).astype(F32)
        rank = mm(below, hits.astype(BF16), NN) + carry
        carry = carry + jnp.sum(hits, axis=0, keepdims=True)
        cols = row[:, k : k + 1].astype(F32)
        for s in range(8):
            sel = jnp.where(rank == s, hits, 0.0)
            picked_r[s] = picked_r[s] + jnp.sum(sel * row1, axis=0, keepdims=True)
            picked_c[s] = picked_c[s] + jnp.sum(sel * cols, axis=0, keepdims=True)
    for s in range(8):
        tbl[0, 0, s : s + 1, :] = picked_r[s].astype(I32)
        tbl[0, 0, 8 + s : 9 + s, :] = picked_c[s].astype(I32)
    for d in (1, 3, 2):
        tbl_y(d).start()

    for d in (1, 3, 2):
        got_a(0, d)
        for e in (1, 3, 2):
            img_a(0, d, e, 0).start()
        got_b(d, 0)
        for e in (1, 3, 2):
            img_b(d, 0, 0, e).start()
        tbl_y(d).wait_recv()
    for d in (1, 3, 2):
        tbl_z(d).start()
    tgrad[...] = jnp.zeros_like(tgrad)
    for d in (1, 3, 2):
        along_x(txt, t_s, t_r, d).wait_recv()
        to_sib(txt, t_s, t_r, d).start()
        along_x(cac, c_s, c_r, d).start()
    to_sib(cac, c_s, c_r, 0).start()
    for d in range(4):
        to_sib(txt, t_s, t_r, d).wait_recv()
    for d in (1, 2, 3):
        tbl_z(d).wait_recv()

    scale = jnp.exp(ls_ref[...])
    half = 0.5 * scale
    shift = 0.5 * bias_ref[...]

    def place(i):
        q, p = i // 2, i % 2
        return q + q // 2 - 2 * (q // 3), p

    def text_step(i):
        dz, p = place(i)
        for j in (0, 1):
            dy = 2 * p + j

            @pl.when(dz != 0)
            def _():
                got_a(dz, dy)

            @pl.when(dy != 0)
            def _():
                got_b(dz, dy)

        pair = dz * 2 + p
        mine = img[pl.ds(pair * 2, 2)].reshape(2 * ROWS, D)
        logit = mm(mine, txt[...], NT)
        coeff[...] = (half + half * jnp.tanh(half * logit + shift)).astype(BF16)

        @pl.when(i == 0)
        def _():
            own = mm(img[0], txt[0:ROWS], NT)
            prob = half + half * jnp.tanh(half * own + shift)
            coeff[0:ROWS, 0:ROWS] = (prob - jnp.where(sub == lane, scale, 0.0)).astype(BF16)

        co = coeff[...]
        part[pl.ds(pair * 2, 2)] = mm(co, txt[...], NN).reshape(2, ROWS, D)
        tgrad[...] += mm(co, mine, TN)

    def spread_lanes(table, first):
        want = lax.broadcasted_iota(I32, (ROWS, ROWS), 0)
        b = lax.broadcasted_iota(I32, (ROWS, ROWS), 1) // 16
        of = first + ((x + b // 2) % 4) * 2 + (c + b) % 2
        return mm(table, (want == of).astype(BF16), NN)

    first = (z * 4 + y) * 8
    tab = tbl[...].reshape(16, 2, 8, ROWS)
    tab_r = tab[:, 0].reshape(ROWS, ROWS).astype(F32).astype(BF16)
    tab_c = tab[:, 1].reshape(ROWS, ROWS).astype(F32).astype(BF16)

    def column(b):
        of = first + ((x + b // 2) % 4) * 2 + (c + b) % 2
        want = lax.broadcasted_iota(I32, (ROWS, ROWS), 0)
        return (mm(tab_c, (want == of).astype(BF16), NN) == lane.astype(F32)).astype(BF16)

    lanes_r = spread_lanes(tab_r, first)

    def gather_rows():
        for d in (1, 3, 2):
            along_x(cac, c_s, c_r, d).wait_recv()
            to_sib(cac, c_s, c_r, d).start()
        for d in range(4):
            to_sib(cac, c_s, c_r, d).wait_recv()
        for b in range(8):
            gat[b] = mm(column(b), cac[pl.ds(b * ROWS, ROWS)], NN).astype(BF16)

    def a1(dz, dy):
        return rc(pbf.at[dz * 4 + dy, LO], ra1.at[dz, dy], ra1_s.at[dz, dy], ra1_r.at[dz, dy], dev(dz))

    def b1(dz, dy):
        return rc(pbf.at[dz * 4 + dy, HI], rb1.at[dy, dz], rb1_s.at[dz, dy], rb1_r.at[dz, dy], dev(0, dy))

    def mate_step(i):
        dz, p = place(i)
        pair = dz * 2 + p
        mine = img[pl.ds(pair * 2, 2)].reshape(2 * ROWS, D)
        emb = gat[:, pl.ds(pair * 16, 16), :].reshape(ROWS, D)
        keep = jnp.where(sub == pair * 16 + lane % 16, lanes_r, 0.0)
        at_row = jnp.sum(keep, axis=0, keepdims=True)
        big_sub = lax.broadcasted_iota(I32, (2 * ROWS, ROWS), 0)
        second = lax.broadcasted_iota(I32, (1, ROWS), 1) % 16 // 8
        target = jnp.where(at_row > 0.5, at_row - 1.0 + second.astype(F32) * ROWS, -1.0)
        named = big_sub.astype(F32) == target
        logit = mm(mine, emb, NT)
        wt = jnp.where(named, half * jnp.tanh(half * logit + shift) - half, 0.0).astype(BF16)
        total = part[pl.ds(pair * 2, 2)].reshape(2 * ROWS, D) + mm(wt, emb, NN)
        part[pl.ds(pair * 2, 2)] = total.reshape(2, ROWS, D)
        pbf[pl.ds(pair * 2, 2)] = total.astype(BF16).reshape(2, ROWS, D)
        slots = mm(wt, mine, TN)
        top = slots.astype(BF16)
        sgr[:, 0, pl.ds(pair * 16, 16), :] = top.reshape(8, 16, D)
        sgr[:, 1, pl.ds(pair * 16, 16), :] = (slots - top.astype(F32)).astype(BF16).reshape(8, 16, D)
        for j in (0, 1):
            dy = 2 * p + j

            @pl.when(dz != 0)
            def _():
                a1(dz, dy).start()

            @pl.when(dy != 0)
            def _():
                b1(dz, dy).start()

    lag = 3

    def step(i, carried):
        @pl.when(i < 8)
        def _():
            text_step(i)

        @pl.when(i == lag)
        def _():
            gather_rows()

        @pl.when(i >= lag)
        def _():
            mate_step(i - lag)

        return carried

    lax.fori_loop(0, 8 + lag, step, 0)

    def sib(buf, rec, base, d):
        return rc(buf.at[d], rec.at[d], x_s.at[base + d], x_r.at[base + d], dev(dc=1))

    def xs(buf, rec, base, d):
        return rc(buf.at[d], rec.at[d], x_s.at[base + d], x_r.at[base + d], dev(dx=d))

    for d in (2, 1, 3, 0):
        tsib[d] = tgrad[pl.ds((2 * d + 1) * ROWS, ROWS)].astype(BF16)
        sib(tsib, trec, 0, d).start()

    def owner_grad(b):
        spots = column(b)
        both = jnp.concatenate([spots, spots], axis=0)
        return mm(both, sgr[b].reshape(2 * ROWS, D), TN)

    for d in (2, 1, 3, 0):
        csib[d] = owner_grad(2 * d + 1).astype(BF16)
        sib(csib, crec, 4, d).start()
    for d in (2, 1, 3):
        sib(tsib, trec, 0, d).wait_recv()
        tsx[d] = (tgrad[pl.ds(2 * d * ROWS, ROWS)] + trec[d].astype(F32)).astype(BF16)
        xs(tsx, trx, 8, d).start()
    for d in (2, 1, 3):
        own = owner_grad(2 * d)
        sib(csib, crec, 4, d).wait_recv()
        csx[d] = (own + crec[d].astype(F32)).astype(BF16)
        xs(csx, crx, 12, d).start()

    def a2(d):
        return rc(sa2.at[d], ra2.at[d], r2_s.at[d], r2_r.at[d], dev(0, d))

    def b2(d):
        return rc(sb2.at[d], rb2.at[d], r2_s.at[4 + d], r2_r.at[4 + d], dev(d))

    for d in (2, 1, 3, 0):
        for e in (1, 2, 3):
            a1(e, d).wait_recv()
            b1(d, e).wait_recv()
        sum_a = part[d, 0:HALF] + ra1[1, d].astype(F32) + ra1[2, d].astype(F32) + ra1[3, d].astype(F32)
        sum_b = part[4 * d, HALF:] + rb1[1, d].astype(F32) + rb1[2, d].astype(F32) + rb1[3, d].astype(F32)
        if d:
            sa2[d] = sum_a.astype(BF16)
            a2(d).start()
            sb2[d] = sum_b.astype(BF16)
            b2(d).start()
        else:
            part[0, 0:HALF] = sum_a
            part[0, HALF:] = sum_b

    sib(tsib, trec, 0, 0).wait_recv()
    for d in (1, 2, 3):
        xs(tsx, trx, 8, d).wait_recv()
    tg_out[...] = (tgrad[0:ROWS] + trec[0].astype(F32) + trx[1].astype(F32) + trx[2].astype(F32) + trx[3].astype(F32))
    own = owner_grad(0)
    sib(csib, crec, 4, 0).wait_recv()
    for d in (1, 2, 3):
        xs(csx, crx, 12, d).wait_recv()
    cg_out[...] = own + crec[0].astype(F32) + crx[1].astype(F32) + crx[2].astype(F32) + crx[3].astype(F32)
    for d in (1, 2, 3):
        a2(d).wait_recv()
        b2(d).wait_recv()
    ig_out[0:HALF] = part[0, 0:HALF] + ra2[1].astype(F32) + ra2[2].astype(F32) + ra2[3].astype(F32)
    ig_out[HALF:] = part[0, HALF:] + rb2[1].astype(F32) + rb2[2].astype(F32) + rb2[3].astype(F32)

    for d in (1, 2, 3):
        for e in range(4):
            img_a(0, e, d, 0).wait_send()
            img_b(e, 0, 0, d).wait_send()
            a1(d, e).wait_send()
            b1(e, d).wait_send()
        img_a(0, 0, 0, d).wait_send()
        img_b(0, 0, d, 0).wait_send()
        for ref, ss, sr in ((txt, t_s, t_r), (cac, c_s, c_r)):
            along_x(ref, ss, sr, d).wait_send()
        tbl_y(d).wait_send()
        tbl_z(d).wait_send()
        xs(tsx, trx, 8, d).wait_send()
        xs(csx, crx, 12, d).wait_send()
        a2(d).wait_send()
        b2(d).wait_send()
    for d in range(4):
        to_sib(txt, t_s, t_r, d).wait_send()
        to_sib(cac, c_s, c_r, d).wait_send()
        sib(tsib, trec, 0, d).wait_send()
        sib(csib, crec, 4, d).wait_send()


def shards(images, texts, cache, mate_owner, mate_row, mate_count, log_scale, bias):
    vm = pl.BlockSpec(memory_space=pltpu.VMEM)
    dma = pltpu.SemaphoreType.DMA
    out = jax.ShapeDtypeStruct((ROWS, D), F32)
    four = lambda rows: pltpu.VMEM((4, rows, D), BF16)
    return tuple(
        pl.pallas_call(
            kernel,
            out_shape=(out, out, out),
            in_specs=[vm] * 8,
            out_specs=(vm, vm, vm),
            scratch_shapes=[
                pltpu.VMEM((16, ROWS, D), BF16),
                pltpu.VMEM((8 * ROWS, D), BF16),
                pltpu.VMEM((8 * ROWS, D), BF16),
                pltpu.VMEM((8, ROWS, D), BF16),
                pltpu.VMEM((4, 4, 16, ROWS), I32),
                pltpu.VMEM((2 * ROWS, 8 * ROWS), BF16),
                pltpu.VMEM((8 * ROWS, D), F32),
                pltpu.VMEM((16, ROWS, D), F32),
                pltpu.VMEM((16, ROWS, D), BF16),
                pltpu.VMEM((8, 2, ROWS, D), BF16),
                pltpu.VMEM((4, 4, HALF, D), BF16),
                pltpu.VMEM((4, 4, HALF, D), BF16),
                four(HALF), four(HALF), four(HALF), four(HALF),
                four(ROWS), four(ROWS), four(ROWS), four(ROWS),
                four(ROWS), four(ROWS), four(ROWS), four(ROWS),
                dma((4, 4)), dma((4, 4)), dma((4, 4)), dma((4, 4)),
                dma((8,)), dma((8,)), dma((8,)), dma((8,)),
                dma((8,)), dma((8,)),
                dma((4, 4)), dma((4, 4)), dma((4, 4)), dma((4, 4)),
                dma((8,)), dma((8,)), dma((16,)), dma((16,)),
            ],
            compiler_params=pltpu.CompilerParams(
                collective_id=0, has_side_effects=True, vmem_limit_bytes=62 << 20
            ),
            cost_estimate=pl.CostEstimate(flops=17_000_000_000, bytes_accessed=4_000_000, transcendentals=2_000_000),
        )(
            log_scale.reshape(1, 1), bias.reshape(1, 1), images, texts, cache,
            mate_owner, mate_row, mate_count.reshape(1, ROWS),
        )
    )


def solution(mesh):
    rows = P(("blk", "img"), None)
    return jax.shard_map(
        shards,
        mesh=mesh,
        in_specs=(rows, rows, rows, rows, rows, P(("blk", "img")), P(), P()),
        out_specs=(rows, rows, rows),
        check_vma=False,
    )
```

```python
import jax
import jax.numpy as jnp
from jax import lax
from jax.experimental import pallas as pl
from jax.experimental.pallas import tpu as pltpu
from jax.sharding import PartitionSpec as P

MESH = pl.DeviceIdType.MESH
F32, BF16, I32 = jnp.float32, jnp.bfloat16, jnp.int32
NT = (((1,), (1,)), ((), ()))
NN = (((1,), (0,)), ((), ()))
TN = (((0,), (0,)), ((), ()))
ROWS, D, HALF, QTR = 128, 1152, 64, 32
LO, HI = pl.ds(0, HALF), pl.ds(HALF, HALF)
QUARTERS = tuple(pl.ds(q * QTR, QTR) for q in range(4))


def mm(a, b, dims):
    return lax.dot_general(a, b, dims, preferred_element_type=F32)


def kernel(
    ls_ref, bias_ref, images, texts, cache, owner, row, count,
    ig_out, tg_out, cg_out,
    img, txt, cac, gat, tbl, coeff, tgrad, part, pbf, sgr,
    rqa, rqb, rha, rhb, usend, uq, uh, tsib, trec, csib, crec, tsx, trx, csx, crx,
    a_s, a_r, b_s, b_r, aq_s, aq_r, bq_s, bq_r, t_s, t_r, c_s, c_r, k_s, k_r,
    rqa_s, rqa_r, rqb_s, rqb_r, rha_s, rha_r, rhb_s, rhb_r, u_s, u_r, x_s, x_r,
):
    blk, im = lax.axis_index("blk"), lax.axis_index("img")
    z, y, x, c = blk // 8, (blk // 2) % 4, (blk % 2) * 2 + im // 2, im % 2

    def dev(dz=0, dy=0, dx=0, dc=0):
        zz, yy, xx = (z + dz + 4) % 4, (y + dy + 4) % 4, (x + dx + 4) % 4
        return ((zz * 4 + yy) * 2 + xx // 2, (xx % 2) * 2 + (c + dc) % 2)

    def rc(src, dst, ss, rs, to):
        return pltpu.make_async_remote_copy(
            src_ref=src, dst_ref=dst, send_sem=ss, recv_sem=rs, device_id=to, device_id_type=MESH
        )

    def blk_a(n):
        return img.at[n, LO]

    def blk_b(n):
        return img.at[n, HI]

    def a_y(d):
        return rc(blk_a(0), blk_a(d), a_s.at[0, d], a_r.at[0, d], dev(0, -d))

    def b_z(d):
        return rc(blk_b(0), blk_b(4 * d), b_s.at[d, 0], b_r.at[d, 0], dev(-d))

    def a_z(dy, d):
        return rc(blk_a(dy), blk_a(4 * d + dy), a_s.at[d, dy], a_r.at[d, dy], dev(-d))

    def b_y(dz, d):
        return rc(blk_b(4 * dz), blk_b(4 * dz + d), b_s.at[dz, d], b_r.at[dz, d], dev(0, -d))

    def aq_y(d):
        q = QUARTERS[d // 2]
        return rc(img.at[d, q], img.at[2, q], aq_s.at[d // 2, 4], aq_r.at[d // 2, 4], dev(0, -d))

    def bq_z(d):
        q = QUARTERS[2 + d // 2]
        return rc(img.at[4 * d, q], img.at[8, q], bq_s.at[d // 2, 4], bq_r.at[d // 2, 4], dev(-d))

    def aq_z(dy, d):
        q = QUARTERS[d // 2]
        return rc(img.at[4 * d + dy, q], img.at[8 + dy, q], aq_s.at[d // 2, dy], aq_r.at[d // 2, dy], dev(-d))

    def bq_y(dz, d):
        q = QUARTERS[2 + d // 2]
        return rc(img.at[4 * dz + d, q], img.at[4 * dz + 2, q], bq_s.at[d // 2, dz], bq_r.at[d // 2, dz], dev(0, -d))

    def rows_of(ref, n):
        return ref.at[pl.ds(n * ROWS, ROWS)]

    def along_x(ref, sems, semr, d):
        return rc(rows_of(ref, 0), rows_of(ref, 2 * d), sems.at[2 * d], semr.at[2 * d], dev(dx=-d))

    def half_x(ref, sems, semr, d):
        h = d // 2 * HALF
        return rc(ref.at[pl.ds(2 * d * ROWS + h, HALF)], ref.at[pl.ds(4 * ROWS + h, HALF)],
                  sems.at[8 + d], semr.at[8 + d], dev(dx=-d))

    def to_sib(ref, sems, semr, d):
        return rc(rows_of(ref, 2 * d), rows_of(ref, 2 * d + 1), sems.at[2 * d + 1], semr.at[2 * d + 1], dev(dc=1))

    def tbl_y(d):
        return rc(tbl.at[0, 0], tbl.at[0, d], k_s.at[d], k_r.at[d], dev(0, -d))

    def tbl_y2():
        return rc(tbl.at[0, 1], tbl.at[0, 2], k_s.at[2], k_r.at[2], dev(0, -1))

    def tbl_z(d):
        return rc(tbl.at[0], tbl.at[d], k_s.at[4 + d], k_r.at[4 + d], dev(-d))

    def tbl_z2():
        return rc(tbl.at[1], tbl.at[2], k_s.at[6], k_r.at[6], dev(-1))

    peers = [dev(dy=1), dev(dy=3), dev(dz=1), dev(dz=3), dev(dx=1), dev(dx=3), dev(dc=1)]
    barrier = pltpu.get_barrier_semaphore()
    for to in peers:
        pl.semaphore_signal(barrier, inc=1, device_id=to, device_id_type=MESH)
    img[0] = images[...]
    txt[0:ROWS] = texts[...]
    cac[0:ROWS] = cache[...]
    pl.semaphore_wait(barrier, len(peers))

    for d in (1, 3):
        a_y(d).start()
        b_z(d).start()
        along_x(txt, t_s, t_r, d).start()
    to_sib(txt, t_s, t_r, 0).start()
    for d in (1, 3):
        b_y(0, d).start()
        a_z(0, d).start()

    lane = lax.broadcasted_iota(I32, (ROWS, ROWS), 1)
    sub = lax.broadcasted_iota(I32, (ROWS, ROWS), 0)
    below = (sub > lane).astype(BF16)

    def down(line):
        return jnp.transpose(jnp.broadcast_to(line.astype(F32), (ROWS, ROWS)))

    live = down(count[...])
    carry = jnp.zeros((1, ROWS), F32)
    picked_r = [jnp.zeros((1, ROWS), F32) for _ in range(8)]
    picked_c = [jnp.zeros((1, ROWS), F32) for _ in range(8)]
    row1 = (sub + 1).astype(F32)
    for k in range(4):
        hits = ((down(owner[k : k + 1, :]) == lane.astype(F32)) & (live > k)).astype(F32)
        rank = mm(below, hits.astype(BF16), NN) + carry
        carry = carry + jnp.sum(hits, axis=0, keepdims=True)
        cols = down(row[k : k + 1, :])
        for s in range(8):
            sel = jnp.where(rank == s, hits, 0.0)
            picked_r[s] = picked_r[s] + jnp.sum(sel * row1, axis=0, keepdims=True)
            picked_c[s] = picked_c[s] + jnp.sum(sel * cols, axis=0, keepdims=True)
    for s in range(8):
        tbl[0, 0, s : s + 1, :] = picked_r[s].astype(I32)
        tbl[0, 0, 8 + s : 9 + s, :] = picked_c[s].astype(I32)
    for d in (1, 3):
        tbl_y(d).start()

    for d in (1, 3):
        a_y(d).wait_recv()
        aq_y(d).start()
        for e in (1, 3):
            a_z(d, e).start()
        b_z(d).wait_recv()
        bq_z(d).start()
        for e in (1, 3):
            b_y(d, e).start()
    for d in (1, 3):
        tbl_y(d).wait_recv()
        if d == 1:
            tbl_y2().start()
    for d in (1, 3):
        b_y(0, d).wait_recv()
        bq_y(0, d).start()
        a_z(0, d).wait_recv()
        aq_z(0, d).start()
    tbl_y2().wait_recv()
    for d in (1, 3):
        tbl_z(d).start()
    tgrad[...] = jnp.zeros_like(tgrad)
    for d in (1, 3):
        along_x(txt, t_s, t_r, d).wait_recv()
        half_x(txt, t_s, t_r, d).start()
        to_sib(txt, t_s, t_r, d).start()
    for d in (1, 3):
        along_x(cac, c_s, c_r, d).start()
    to_sib(cac, c_s, c_r, 0).start()
    for d in (1, 3):
        aq_y(d).wait_recv()
        bq_z(d).wait_recv()
    for d in (1, 3):
        a_z(2, d).start()
        b_y(2, d).start()
    for d in (1, 3):
        tbl_z(d).wait_recv()
        if d == 1:
            tbl_z2().start()
    for d in (1, 3):
        half_x(txt, t_s, t_r, d).wait_recv()
    to_sib(txt, t_s, t_r, 2).start()

    def corners():
        for e in (1, 3):
            for d in (1, 3):
                a_z(e, d).wait_recv()
                aq_z(e, d).start()
                b_y(e, d).wait_recv()
                bq_y(e, d).start()

    def edges():
        for d in (1, 3):
            a_z(2, d).wait_recv()
            aq_z(2, d).start()
            b_y(2, d).wait_recv()
            bq_y(2, d).start()

    def cache_near():
        for d in (1, 3):
            along_x(cac, c_s, c_r, d).wait_recv()
            half_x(cac, c_s, c_r, d).start()
            to_sib(cac, c_s, c_r, d).start()

    def cache_far():
        for d in (1, 3):
            half_x(cac, c_s, c_r, d).wait_recv()
        to_sib(cac, c_s, c_r, 2).start()

    def last_dz0():
        for d in (1, 3):
            bq_y(0, d).wait_recv()

    def last_dz(e):
        for d in (1, 3):
            bq_y(e, d).wait_recv()

    def last_quarters():
        for e in range(4):
            for d in (1, 3):
                aq_z(e, d).wait_recv()
        last_dz(2)

    for d in range(4):
        to_sib(txt, t_s, t_r, d).wait_recv()
    tbl_z2().wait_recv()

    scale = jnp.exp(ls_ref[...])
    half = 0.5 * scale
    shift = 0.5 * bias_ref[...]

    def place(i):
        q, p = i // 2, i % 2
        return q + q // 2 - 2 * (q // 3), p

    def text_step(i):
        dz, p = place(i)
        pair = dz * 2 + p
        mine = img[pl.ds(pair * 2, 2)].reshape(2 * ROWS, D)
        logit = mm(mine, txt[...], NT)
        coeff[...] = (half + half * jnp.tanh(half * logit + shift)).astype(BF16)

        @pl.when(i == 0)
        def _():
            own = mm(img[0], txt[0:ROWS], NT)
            prob = half + half * jnp.tanh(half * own + shift)
            coeff[0:ROWS, 0:ROWS] = (prob - jnp.where(sub == lane, scale, 0.0)).astype(BF16)

        co = coeff[...]
        part[pl.ds(pair * 2, 2)] = mm(co, txt[...], NN).reshape(2, ROWS, D)
        tgrad[...] += mm(co, mine, TN)

    def spread_lanes(table, first):
        want = lax.broadcasted_iota(I32, (ROWS, ROWS), 0)
        b = lax.broadcasted_iota(I32, (ROWS, ROWS), 1) // 16
        of = first + ((x + b // 2) % 4) * 2 + (c + b) % 2
        return mm(table, (want == of).astype(BF16), NN)

    first = (z * 4 + y) * 8
    tab = tbl[...].reshape(16, 2, 8, ROWS)
    tab_r = tab[:, 0].reshape(ROWS, ROWS).astype(F32).astype(BF16)
    tab_c = tab[:, 1].reshape(ROWS, ROWS).astype(F32).astype(BF16)

    def column(b):
        of = first + ((x + b // 2) % 4) * 2 + (c + b) % 2
        want = lax.broadcasted_iota(I32, (ROWS, ROWS), 0)
        return (mm(tab_c, (want == of).astype(BF16), NN) == lane.astype(F32)).astype(BF16)

    lanes_r = spread_lanes(tab_r, first)

    def gather_rows():
        for d in range(4):
            to_sib(cac, c_s, c_r, d).wait_recv()
        for b in range(8):
            gat[b] = mm(column(b), cac[pl.ds(b * ROWS, ROWS)], NN).astype(BF16)

    def far_a(dy, d):
        q = QUARTERS[d // 2]
        return rc(pbf.at[8 + dy, q], rqa.at[d // 2, dy], rqa_s.at[d // 2, dy], rqa_r.at[d // 2, dy], dev(d))

    def far_b(dz, d):
        q = QUARTERS[2 + d // 2]
        return rc(pbf.at[4 * dz + 2, q], rqb.at[d // 2, dz], rqb_s.at[d // 2, dz], rqb_r.at[d // 2, dz], dev(0, d))

    def near_a(dy, d):
        return rc(pbf.at[4 * d + dy, LO], rha.at[d // 2, dy], rha_s.at[d // 2, dy], rha_r.at[d // 2, dy], dev(d))

    def near_b(dz, d):
        return rc(pbf.at[4 * dz + d, HI], rhb.at[d // 2, dz], rhb_s.at[d // 2, dz], rhb_r.at[d // 2, dz], dev(0, d))

    def mate_step(i):
        dz, p = place(i)
        pair = dz * 2 + p
        mine = img[pl.ds(pair * 2, 2)].reshape(2 * ROWS, D)
        emb = gat[:, pl.ds(pair * 16, 16), :].reshape(ROWS, D)
        keep = jnp.where(sub == pair * 16 + lane % 16, lanes_r, 0.0)
        at_row = jnp.sum(keep, axis=0, keepdims=True)
        big_sub = lax.broadcasted_iota(I32, (2 * ROWS, ROWS), 0)
        second = lax.broadcasted_iota(I32, (1, ROWS), 1) % 16 // 8
        target = jnp.where(at_row > 0.5, at_row - 1.0 + second.astype(F32) * ROWS, -1.0)
        named = big_sub.astype(F32) == target
        logit = mm(mine, emb, NT)
        wt = jnp.where(named, half * jnp.tanh(half * logit + shift) - half, 0.0).astype(BF16)
        total = part[pl.ds(pair * 2, 2)].reshape(2 * ROWS, D) + mm(wt, emb, NN)
        part[pl.ds(pair * 2, 2)] = total.reshape(2, ROWS, D)
        pbf[pl.ds(pair * 2, 2)] = total.astype(BF16).reshape(2, ROWS, D)
        slots = mm(wt, mine, TN)
        top = slots.astype(BF16)
        sgr[:, 0, pl.ds(pair * 16, 16), :] = top.reshape(8, 16, D)
        sgr[:, 1, pl.ds(pair * 16, 16), :] = (slots - top.astype(F32)).astype(BF16).reshape(8, 16, D)
        for d in (1, 3):
            @pl.when(dz == 2)
            def _():
                far_a(2 * p, d).start()
                far_a(2 * p + 1, d).start()

            @pl.when(p == 1)
            def _():
                far_b(dz, d).start()

    lag = 4

    def step(i, carried):
        @pl.when(i == 2)
        def _():
            corners()

        @pl.when(i == 1)
        def _():
            last_dz0()

        @pl.when(i == 3)
        def _():
            edges()
            cache_near()
            last_dz(1)

        @pl.when(i == 4)
        def _():
            last_dz(3)

        @pl.when(i == 6)
        def _():
            last_quarters()

        @pl.when(i < 8)
        def _():
            text_step(i)

        @pl.when(i == lag)
        def _():
            cache_far()
            gather_rows()

        @pl.when(i >= lag)
        def _():
            mate_step(i - lag)

        return carried

    lax.fori_loop(0, 8 + lag, step, 0)

    def near_sends(e):
        for d in (1, 3):
            far_a(e, d).wait_recv()
            q = d // 2 * QTR
            pbf[4 * d + e, q : q + QTR] = (part[4 * d + e, q : q + QTR] + rqa[d // 2, e].astype(F32)).astype(BF16)
            near_a(e, d).start()
            far_b(e, d).wait_recv()
            q = HALF + d // 2 * QTR
            pbf[4 * e + d, q : q + QTR] = (part[4 * e + d, q : q + QTR] + rqb[d // 2, e].astype(F32)).astype(BF16)
            near_b(e, d).start()

    for e in (2, 1, 3, 0):
        near_sends(e)

    def sib(buf, rec, base, d):
        return rc(buf.at[d], rec.at[d], x_s.at[base + d], x_r.at[base + d], dev(dc=1))

    def xfar(buf, rec, base, d):
        h = pl.ds(d // 2 * HALF, HALF)
        return rc(buf.at[2, h], rec.at[0, h], x_s.at[base + d], x_r.at[base + d], dev(dx=d))

    def xnear(buf, rec, base, d):
        return rc(buf.at[d], rec.at[d], x_s.at[base + 3 + d], x_r.at[base + 3 + d], dev(dx=d))

    for d in (2, 1, 3, 0):
        tsib[d] = tgrad[pl.ds((2 * d + 1) * ROWS, ROWS)].astype(BF16)
        sib(tsib, trec, 0, d).start()

    def owner_grad(b):
        spots = column(b)
        both = jnp.concatenate([spots, spots], axis=0)
        return mm(both, sgr[b].reshape(2 * ROWS, D), TN)

    for d in (2, 1, 3):
        sib(tsib, trec, 0, d).wait_recv()
        share = tgrad[pl.ds(2 * d * ROWS, ROWS)] + trec[d].astype(F32)
        if d == 2:
            tsx[2] = share.astype(BF16)
            for e in (1, 3):
                xfar(tsx, trx, 8, e).start()
        else:
            tgrad[pl.ds(2 * d * ROWS, ROWS)] = share
    for d in (2, 1, 3, 0):
        csib[d] = owner_grad(2 * d + 1).astype(BF16)
        sib(csib, crec, 4, d).start()
    own_c = {}
    for d in (2, 1, 3):
        own_c[d] = owner_grad(2 * d)
        sib(csib, crec, 4, d).wait_recv()
        own_c[d] = own_c[d] + crec[d].astype(F32)
        if d == 2:
            csx[2] = own_c[2].astype(BF16)
            for e in (1, 3):
                xfar(csx, crx, 16, e).start()
    for d in (1, 3):
        xfar(tsx, trx, 8, d).wait_recv()
        h = d // 2 * HALF
        tsx[d] = tgrad[pl.ds(2 * d * ROWS, ROWS)].astype(BF16)
        tsx[d, h : h + HALF] = (tgrad[pl.ds(2 * d * ROWS + h, HALF)] + trx[0, h : h + HALF].astype(F32)).astype(BF16)
        xnear(tsx, trx, 8, d).start()
    for d in (1, 3):
        xfar(csx, crx, 16, d).wait_recv()
        h = d // 2 * HALF
        csx[d] = own_c[d].astype(BF16)
        csx[d, h : h + HALF] = (own_c[d][h : h + HALF] + crx[0, h : h + HALF].astype(F32)).astype(BF16)
        xnear(csx, crx, 16, d).start()

    def line(w, d):
        return dev(0, d) if w == 0 else dev(d)

    def ufar(w, d):
        q = pl.ds(d // 2 * QTR, QTR)
        return rc(usend.at[w, 2, q], uq.at[w, q], u_s.at[w, d], u_r.at[w, d], line(w, d))

    def unear(w, d):
        return rc(usend.at[w, d], uh.at[w, d], u_s.at[w, 4 + d], u_r.at[w, 4 + d], line(w, d))

    for e in (2, 1, 3, 0):
        for w in (0, 1):
            at, top = (e, 0) if w == 0 else (4 * e, HALF)
            near, rec = (near_a, rha) if w == 0 else (near_b, rhb)
            for d in (1, 3):
                near(e, d).wait_recv()
            total = part[at, top : top + HALF] + rec[0, e].astype(F32) + rec[1, e].astype(F32)
            if e == 2:
                usend[w, 2] = total.astype(BF16)
                for d in (1, 3):
                    ufar(w, d).start()
            elif e:
                ufar(w, e).wait_recv()
                usend[w, e] = total.astype(BF16)
                q = e // 2 * QTR
                usend[w, e, q : q + QTR] = (total[q : q + QTR] + uq[w, q : q + QTR].astype(F32)).astype(BF16)
                unear(w, e).start()
            else:
                part[0, top : top + HALF] = total

    sib(tsib, trec, 0, 0).wait_recv()
    for d in (1, 3):
        xnear(tsx, trx, 8, d).wait_recv()
    tg_out[...] = tgrad[0:ROWS] + trec[0].astype(F32) + trx[1].astype(F32) + trx[3].astype(F32)
    own = owner_grad(0)
    sib(csib, crec, 4, 0).wait_recv()
    for d in (1, 3):
        xnear(csx, crx, 16, d).wait_recv()
    cg_out[...] = own + crec[0].astype(F32) + crx[1].astype(F32) + crx[3].astype(F32)
    for w in (0, 1):
        for d in (1, 3):
            unear(w, d).wait_recv()
        top = w * HALF
        ig_out[top : top + HALF] = part[0, top : top + HALF] + uh[w, 1].astype(F32) + uh[w, 3].astype(F32)

    for d in (1, 3):
        a_y(d).wait_send()
        b_z(d).wait_send()
        aq_y(d).wait_send()
        bq_z(d).wait_send()
        for e in range(4):
            a_z(e, d).wait_send()
            b_y(e, d).wait_send()
            aq_z(e, d).wait_send()
            bq_y(e, d).wait_send()
            far_a(e, d).wait_send()
            far_b(e, d).wait_send()
            near_a(e, d).wait_send()
            near_b(e, d).wait_send()
        for ref, ss, sr in ((txt, t_s, t_r), (cac, c_s, c_r)):
            along_x(ref, ss, sr, d).wait_send()
            half_x(ref, ss, sr, d).wait_send()
        tbl_y(d).wait_send()
        tbl_z(d).wait_send()
        for buf, rec, base in ((tsx, trx, 8), (csx, crx, 16)):
            xfar(buf, rec, base, d).wait_send()
            xnear(buf, rec, base, d).wait_send()
        for w in (0, 1):
            ufar(w, d).wait_send()
            unear(w, d).wait_send()
    tbl_y2().wait_send()
    tbl_z2().wait_send()
    for d in range(4):
        to_sib(txt, t_s, t_r, d).wait_send()
        to_sib(cac, c_s, c_r, d).wait_send()
        sib(tsib, trec, 0, d).wait_send()
        sib(csib, crec, 4, d).wait_send()


def place_out(a, b, c, a_out, b_out, c_out, held, sems):
    ways = tuple(enumerate(((a, a_out), (b, b_out), (c, c_out))))
    into = [pltpu.make_async_copy(s, held.at[n], sems.at[n]) for n, (s, _) in ways]
    out = [pltpu.make_async_copy(held.at[n], t, sems.at[3 + n]) for n, (_, t) in ways]
    for copy in into:
        copy.start()
    for first, then in zip(into, out):
        first.wait()
        then.start()
    for copy in out:
        copy.wait()


def shards(images, texts, cache, mate_owner, mate_row, mate_count, log_scale, bias):
    vm = pl.BlockSpec(memory_space=pltpu.VMEM)
    dma = pltpu.SemaphoreType.DMA
    out = jax.ShapeDtypeStruct((ROWS, D), F32)
    four = lambda rows: pltpu.VMEM((4, rows, D), BF16)
    grads = (
        pl.pallas_call(
            kernel,
            out_shape=(out, out, out),
            in_specs=[vm] * 8,
            out_specs=(vm, vm, vm),
            scratch_shapes=[
                pltpu.VMEM((16, ROWS, D), BF16),
                pltpu.VMEM((8 * ROWS, D), BF16),
                pltpu.VMEM((8 * ROWS, D), BF16),
                pltpu.VMEM((8, ROWS, D), BF16),
                pltpu.VMEM((4, 4, 16, ROWS), I32),
                pltpu.VMEM((2 * ROWS, 8 * ROWS), BF16),
                pltpu.VMEM((8 * ROWS, D), F32),
                pltpu.VMEM((16, ROWS, D), F32),
                pltpu.VMEM((16, ROWS, D), BF16),
                pltpu.VMEM((8, 2, ROWS, D), BF16),
                pltpu.VMEM((2, 4, QTR, D), BF16),
                pltpu.VMEM((2, 4, QTR, D), BF16),
                pltpu.VMEM((2, 4, HALF, D), BF16),
                pltpu.VMEM((2, 4, HALF, D), BF16),
                pltpu.VMEM((2, 4, HALF, D), BF16),
                pltpu.VMEM((2, HALF, D), BF16),
                pltpu.VMEM((2, 4, HALF, D), BF16),
                four(ROWS), four(ROWS), four(ROWS), four(ROWS),
                four(ROWS), four(ROWS), four(ROWS), four(ROWS),
                dma((4, 4)), dma((4, 4)), dma((4, 4)), dma((4, 4)),
                dma((2, 5)), dma((2, 5)), dma((2, 5)), dma((2, 5)),
                dma((12,)), dma((12,)), dma((12,)), dma((12,)),
                dma((8,)), dma((8,)),
                dma((2, 4)), dma((2, 4)), dma((2, 4)), dma((2, 4)),
                dma((2, 4)), dma((2, 4)), dma((2, 4)), dma((2, 4)),
                dma((2, 8)), dma((2, 8)), dma((24,)), dma((24,)),
            ],
            compiler_params=pltpu.CompilerParams(
                collective_id=0, has_side_effects=True, vmem_limit_bytes=62 << 20
            ),
            cost_estimate=pl.CostEstimate(flops=17_000_000_000, bytes_accessed=4_000_000, transcendentals=2_000_000),
        )(
            log_scale.reshape(1, 1), bias.reshape(1, 1), images, texts, cache,
            mate_owner.T, mate_row.T, mate_count.reshape(1, ROWS),
        )
    )
    anywhere = pl.BlockSpec(memory_space=pl.ANY)
    return tuple(
        pl.pallas_call(
            place_out,
            out_shape=(out, out, out),
            in_specs=[anywhere] * 3,
            out_specs=(anywhere,) * 3,
            scratch_shapes=[pltpu.VMEM((3, ROWS, D), F32), dma((6,))],
        )(*grads)
    )


def solution(mesh):
    rows = P(("blk", "img"), None)
    return jax.shard_map(
        shards,
        mesh=mesh,
        in_specs=(rows, rows, rows, rows, rows, P(("blk", "img")), P(), P()),
        out_specs=(rows, rows, rows),
        check_vma=False,
    )
```

```python
import jax
import jax.numpy as jnp
from jax import lax
from jax.experimental import pallas as pl
from jax.experimental.pallas import tpu as pltpu
from jax.sharding import PartitionSpec as P

MESH = pl.DeviceIdType.MESH
F32, BF16, I32 = jnp.float32, jnp.bfloat16, jnp.int32
NT = (((1,), (1,)), ((), ()))
NN = (((1,), (0,)), ((), ()))
TN = (((0,), (0,)), ((), ()))
ROWS, D, HALF, QTR = 128, 1152, 64, 32
ORDER = ((1, 0), (1, 1), (0, 2), (1, 2), (0, 1), (1, 3), (0, 3), (0, 0))
SLAB = {key: n for n, key in enumerate(ORDER)}


def mm(a, b, dims):
    return lax.dot_general(a, b, dims, preferred_element_type=F32)


def kernel(
    ls_ref, bias_ref, images, texts, cache, owner, row, count,
    ig_out, tg_out, cg_out,
    img, txt, cac, gat, tbl, coeff, tgrad, part, pbf, sgr,
    rq, rh, usend, uq, uh, tsib, trec, csib, crec, tsx, trx, csx, crx, cgrad,
    h_s, h_r, q_s, q_r, t_s, t_r, c_s, c_r, k_s, k_r,
    rq_s, rq_r, rh_s, rh_r, u_s, u_r, x_s, x_r,
):
    blk, im = lax.axis_index("blk"), lax.axis_index("img")
    z, y, x, c = blk // 8, (blk // 2) % 4, (blk % 2) * 2 + im // 2, im % 2

    def dev(dz=0, dy=0, dx=0, dc=0):
        zz, yy, xx = (z + dz + 4) % 4, (y + dy + 4) % 4, (x + dx + 4) % 4
        return ((zz * 4 + yy) * 2 + xx // 2, (xx % 2) * 2 + (c + dc) % 2)

    def rc(src, dst, ss, rs, to):
        return pltpu.make_async_remote_copy(
            src_ref=src, dst_ref=dst, send_sem=ss, recv_sem=rs, device_id=to, device_id_type=MESH
        )

    def outer_dev(h, d):
        return dev(d) if h else dev(0, d)

    def inner_dev(h, d):
        return dev(0, d) if h else dev(d)

    def quarter(d):
        return pl.ds(d // 2 * QTR, QTR)

    def go_out(h, d):
        return rc(img.at[SLAB[h, 0], 0], img.at[SLAB[h, d], 0], h_s.at[h, d, 0], h_r.at[h, d, 0], outer_dev(h, -d))

    def go_out_q(h, d):
        q = quarter(d)
        return rc(img.at[SLAB[h, d], 0, q], img.at[SLAB[h, 2], 0, q],
                  q_s.at[h, d // 2, 4], q_r.at[h, d // 2, 4], outer_dev(h, -d))

    def go_in(h, o, d):
        return rc(img.at[SLAB[h, o], 0], img.at[SLAB[h, o], d], h_s.at[h, o, d], h_r.at[h, o, d], inner_dev(h, -d))

    def go_in_q(h, o, d):
        q = quarter(d)
        return rc(img.at[SLAB[h, o], d, q], img.at[SLAB[h, o], 2, q],
                  q_s.at[h, d // 2, o], q_r.at[h, d // 2, o], inner_dev(h, -d))

    def rows_of(ref, n):
        return ref.at[pl.ds(n * ROWS, ROWS)]

    def along_x(ref, sems, semr, d):
        return rc(rows_of(ref, 0), rows_of(ref, 2 * d), sems.at[2 * d], semr.at[2 * d], dev(dx=-d))

    def half_x(ref, sems, semr, d):
        h = d // 2 * HALF
        return rc(ref.at[pl.ds(2 * d * ROWS + h, HALF)], ref.at[pl.ds(4 * ROWS + h, HALF)],
                  sems.at[8 + d], semr.at[8 + d], dev(dx=-d))

    def to_sib(ref, sems, semr, d):
        return rc(rows_of(ref, 2 * d), rows_of(ref, 2 * d + 1), sems.at[2 * d + 1], semr.at[2 * d + 1], dev(dc=1))

    def tbl_to(dz, dy):
        return rc(tbl.at[0, 0], tbl.at[dz, dy], k_s.at[dz, dy], k_r.at[dz, dy], dev(-dz, -dy))

    plane = [(dz, dy) for dz in range(4) for dy in range(4) if dz or dy]
    peers = [dev(dz, dy) for dz, dy in plane] + [dev(dx=1), dev(dx=3), dev(dc=1)]
    barrier = pltpu.get_barrier_semaphore()
    for to in peers:
        pl.semaphore_signal(barrier, inc=1, device_id=to, device_id_type=MESH)
    for h in (0, 1):
        img[SLAB[h, 0], 0] = images[h * HALF : h * HALF + HALF]
    txt[0:ROWS] = texts[...]
    cac[0:ROWS] = cache[...]
    lane = lax.broadcasted_iota(I32, (ROWS, ROWS), 1)
    sub = lax.broadcasted_iota(I32, (ROWS, ROWS), 0)
    below = (sub > lane).astype(BF16)

    def down(line):
        return jnp.transpose(jnp.broadcast_to(line.astype(F32), (ROWS, ROWS)))

    live = down(count[...])
    carry = jnp.zeros((1, ROWS), F32)
    picked_r = [jnp.zeros((1, ROWS), F32) for _ in range(8)]
    picked_c = [jnp.zeros((1, ROWS), F32) for _ in range(8)]
    row1 = (sub + 1).astype(F32)
    for k in range(4):
        hits = ((down(owner[k : k + 1, :]) == lane.astype(F32)) & (live > k)).astype(F32)
        rank = mm(below, hits.astype(BF16), NN) + carry
        carry = carry + jnp.sum(hits, axis=0, keepdims=True)
        cols = down(row[k : k + 1, :])
        for s in range(8):
            sel = jnp.where(rank == s, hits, 0.0)
            picked_r[s] = picked_r[s] + jnp.sum(sel * row1, axis=0, keepdims=True)
            picked_c[s] = picked_c[s] + jnp.sum(sel * cols, axis=0, keepdims=True)
    for s in range(8):
        tbl[0, 0, s : s + 1, :] = picked_r[s].astype(I32)
        tbl[0, 0, 8 + s : 9 + s, :] = picked_c[s].astype(I32)
    pl.semaphore_wait(barrier, len(peers))
    for dz, dy in plane:
        tbl_to(dz, dy).start()

    for d in (1, 3):
        for h in (0, 1):
            go_out(h, d).start()
        along_x(cac, c_s, c_r, d).start()
    to_sib(cac, c_s, c_r, 0).start()
    for d in (1, 3):
        for h in (0, 1):
            go_in(h, 0, d).start()

    for d in (1, 3):
        for h in (0, 1):
            go_out(h, d).wait_recv()
            go_out_q(h, d).start()
            for e in (1, 3):
                go_in(h, d, e).start()
    for d in (1, 3):
        along_x(cac, c_s, c_r, d).wait_recv()
        half_x(cac, c_s, c_r, d).start()
        to_sib(cac, c_s, c_r, d).start()
    for d in (1, 3):
        along_x(txt, t_s, t_r, d).start()
    to_sib(txt, t_s, t_r, 0).start()
    for d in (1, 3):
        for h in (0, 1):
            go_in(h, 0, d).wait_recv()
            go_in_q(h, 0, d).start()
    tgrad[...] = jnp.zeros_like(tgrad)
    for h in (0, 1):
        for d in (1, 3):
            go_out_q(h, d).wait_recv()
        for d in (1, 3):
            go_in(h, 2, d).start()
    for d in (1, 3):
        half_x(cac, c_s, c_r, d).wait_recv()
    to_sib(cac, c_s, c_r, 2).start()
    for dz, dy in plane:
        tbl_to(dz, dy).wait_recv()

    scale = jnp.exp(ls_ref[...])
    half = 0.5 * scale
    shift = 0.5 * bias_ref[...]

    def text_step(t):
        mine = img[t].reshape(2 * ROWS, D)
        logit = mm(mine, txt[...], NT)
        coeff[...] = (half + half * jnp.tanh(half * logit + shift)).astype(BF16)

        for h in (0, 1):
            @pl.when(t == SLAB[h, 0])
            def _():
                own = mm(img[SLAB[h, 0], 0], txt[0:ROWS], NT)
                prob = half + half * jnp.tanh(half * own + shift)
                same = sub[0:HALF] + h * HALF == lane[0:HALF]
                coeff[0:HALF, 0:ROWS] = (prob - jnp.where(same, scale, 0.0)).astype(BF16)

        co = coeff[...]
        total = part[t] + mm(co, txt[...], NN).reshape(4, HALF, D)
        part[t] = total
        pbf[t] = total.astype(BF16)
        tgrad[...] += mm(co, mine, TN)

    def spread_lanes(table, first):
        want = lax.broadcasted_iota(I32, (ROWS, ROWS), 0)
        b = lax.broadcasted_iota(I32, (ROWS, ROWS), 1) // 16
        of = first + ((x + b // 2) % 4) * 2 + (c + b) % 2
        return mm(table, (want == of).astype(BF16), NN)

    first = (z * 4 + y) * 8
    tab = tbl[...].reshape(16, 2, 8, ROWS)
    tab_r = tab[:, 0].reshape(ROWS, ROWS).astype(F32).astype(BF16)
    tab_c = tab[:, 1].reshape(ROWS, ROWS).astype(F32).astype(BF16)

    def column(b):
        of = first + ((x + b // 2) % 4) * 2 + (c + b) % 2
        want = lax.broadcasted_iota(I32, (ROWS, ROWS), 0)
        return (mm(tab_c, (want == of).astype(BF16), NN) == lane.astype(F32)).astype(BF16)

    lanes_r = spread_lanes(tab_r, first)

    def gather_rows():
        for d in range(4):
            to_sib(cac, c_s, c_r, d).wait_recv()
        for b in range(8):
            gat[b] = mm(column(b), cac[pl.ds(b * ROWS, ROWS)], NN).astype(BF16)

    def far(h, o, d):
        return rc(pbf.at[SLAB[h, o], 2, quarter(d)], rq.at[h, d // 2, o],
                  rq_s.at[h, d // 2, o], rq_r.at[h, d // 2, o], inner_dev(h, d))

    def near(h, o, d):
        return rc(pbf.at[SLAB[h, o], d], rh.at[h, d // 2, o],
                  rh_s.at[h, d // 2, o], rh_r.at[h, d // 2, o], inner_dev(h, d))

    def ufar(h, d):
        return rc(usend.at[h, 2, quarter(d)], uq.at[h, quarter(d)], u_s.at[h, d], u_r.at[h, d], outer_dev(h, d))

    def unear(h, d):
        return rc(usend.at[h, d], uh.at[h, d], u_s.at[h, 4 + d], u_r.at[h, 4 + d], outer_dev(h, d))

    def far_sends(h, o):
        for d in (1, 3):
            far(h, o, d).start()

    def near_sends(h, o):
        n = SLAB[h, o]
        for d in (1, 3):
            far(h, o, d).wait_recv()
            q = d // 2 * QTR
            pbf[n, d, q : q + QTR] = (part[n, d, q : q + QTR] + rq[h, d // 2, o].astype(F32)).astype(BF16)
            near(h, o, d).start()

    def inner_sum(h, o):
        n = SLAB[h, o]
        for d in (1, 3):
            near(h, o, d).wait_recv()
        total = part[n, 0] + rh[h, 0, o].astype(F32) + rh[h, 1, o].astype(F32)
        if o == 2:
            usend[h, 2] = total.astype(BF16)
            for d in (1, 3):
                ufar(h, d).start()
        else:
            part[n, 0] = total

    def outer_send(h, o):
        n, q = SLAB[h, o], o // 2 * QTR
        ufar(h, o).wait_recv()
        usend[h, o] = part[n, 0].astype(BF16)
        usend[h, o, q : q + QTR] = (part[n, 0, q : q + QTR] + uq[h, q : q + QTR].astype(F32)).astype(BF16)
        unear(h, o).start()

    def mate_step(dz, p):
        pair = dz * 2 + p
        mine = jnp.concatenate(
            [img[SLAB[0, 2 * p], dz], img[SLAB[0, 2 * p + 1], dz], img[SLAB[1, dz], 2 * p], img[SLAB[1, dz], 2 * p + 1]],
            axis=0,
        )
        emb = gat[:, pair * 16 : pair * 16 + 16, :].reshape(ROWS, D)
        keep = jnp.where(sub == pair * 16 + lane % 16, lanes_r, 0.0)
        at_row = jnp.sum(keep, axis=0, keepdims=True)
        big_sub = lax.broadcasted_iota(I32, (2 * ROWS, ROWS), 0)
        second = lax.broadcasted_iota(I32, (1, ROWS), 1) % 16 // 8
        moved = jnp.where(at_row > HALF + 0.5, 64.0, 0.0) + second.astype(F32) * HALF
        target = jnp.where(at_row > 0.5, at_row - 1.0 + moved, -1.0)
        named = big_sub.astype(F32) == target
        logit = mm(mine, emb, NT)
        wt = jnp.where(named, half * jnp.tanh(half * logit + shift) - half, 0.0).astype(BF16)
        grad = mm(wt, emb, NN)
        part[SLAB[0, 2 * p], dz] = grad[0:HALF]
        part[SLAB[0, 2 * p + 1], dz] = grad[HALF:ROWS]
        part[SLAB[1, dz], 2 * p] = grad[ROWS : ROWS + HALF]
        part[SLAB[1, dz], 2 * p + 1] = grad[ROWS + HALF :]
        slots = mm(wt, mine, TN)
        top = slots.astype(BF16)
        sgr[:, 0, pair * 16 : pair * 16 + 16, :] = top.reshape(8, 16, D)
        sgr[:, 1, pair * 16 : pair * 16 + 16, :] = (slots - top.astype(F32)).astype(BF16).reshape(8, 16, D)
    def in_quarters(h, o):
        for d in (1, 3):
            go_in_q(h, o, d).wait_recv()

    gather_rows()
    mate_step(0, 0)
    for o in (1, 3):
        for h in (0, 1):
            for d in (1, 3):
                go_in(h, o, d).wait_recv()
                go_in_q(h, o, d).start()
    mate_step(1, 0)
    mate_step(3, 0)
    in_quarters(1, 0)
    mate_step(0, 1)
    for d in (1, 3):
        along_x(txt, t_s, t_r, d).wait_recv()
        half_x(txt, t_s, t_r, d).start()
        to_sib(txt, t_s, t_r, d).start()
    for h in (0, 1):
        for d in (1, 3):
            go_in(h, 2, d).wait_recv()
            go_in_q(h, 2, d).start()
    in_quarters(1, 1)
    mate_step(1, 1)
    in_quarters(1, 3)
    mate_step(3, 1)
    for d in (1, 3):
        half_x(txt, t_s, t_r, d).wait_recv()
    to_sib(txt, t_s, t_r, 2).start()
    for d in range(4):
        to_sib(txt, t_s, t_r, d).wait_recv()

    def sib(buf, rec, base, d):
        return rc(buf.at[d], rec.at[d], x_s.at[base + d], x_r.at[base + d], dev(dc=1))

    def xfar(buf, rec, base, d):
        h = pl.ds(d // 2 * HALF, HALF)
        return rc(buf.at[2, h], rec.at[0, h], x_s.at[base + d], x_r.at[base + d], dev(dx=d))

    def xnear(buf, rec, base, d):
        return rc(buf.at[d], rec.at[d], x_s.at[base + 3 + d], x_r.at[base + 3 + d], dev(dx=d))

    def owner_grad(b):
        spots = column(b)
        both = jnp.concatenate([spots, spots], axis=0)
        return mm(both, sgr[b].reshape(2 * ROWS, D), TN)

    def cache_to_sibling():
        for d in (2, 1, 3, 0):
            csib[d] = owner_grad(2 * d + 1).astype(BF16)
            sib(csib, crec, 4, d).start()

    def cache_far_sends():
        for d in (2, 1, 3, 0):
            cgrad[d] = owner_grad(2 * d)
            sib(csib, crec, 4, d).wait_recv()
            cgrad[d] += crec[d].astype(F32)
            if d == 2:
                csx[2] = cgrad[2].astype(BF16)
                for e in (1, 3):
                    xfar(csx, crx, 16, e).start()

    def cache_near_sends():
        for d in (1, 3):
            xfar(csx, crx, 16, d).wait_recv()
            h = d // 2 * HALF
            csx[d] = cgrad[d].astype(BF16)
            csx[d, h : h + HALF] = (cgrad[d, h : h + HALF] + crx[0, h : h + HALF].astype(F32)).astype(BF16)
            xnear(csx, crx, 16, d).start()

    def cache_result():
        for d in (1, 3):
            xnear(csx, crx, 16, d).wait_recv()
        cg_out[...] = cgrad[0] + crx[1].astype(F32) + crx[3].astype(F32)

    def step(t, carried):
        @pl.when(t == 2)
        def _():
            in_quarters(0, 0)
            in_quarters(0, 1)
            mate_step(2, 0)
            in_quarters(0, 2)
            in_quarters(0, 3)
            in_quarters(1, 2)
            mate_step(2, 1)
            cache_to_sibling()

        text_step(t)
        for n in range(8):
            @pl.when(t == n)
            def _():
                far_sends(*ORDER[n])
                if n >= 2:
                    near_sends(*ORDER[n - 2])
                if n == 2:
                    cache_far_sends()
                if n >= 4:
                    inner_sum(*ORDER[n - 4])
                if n == 4:
                    cache_near_sends()

        return carried

    lax.fori_loop(0, 8, step, 0)

    for d in (2, 1, 3, 0):
        tsib[d] = tgrad[(2 * d + 1) * ROWS : (2 * d + 2) * ROWS].astype(BF16)
        sib(tsib, trec, 0, d).start()
    near_sends(*ORDER[6])
    inner_sum(*ORDER[4])
    outer_send(0, 1)
    sib(tsib, trec, 0, 2).wait_recv()
    tsx[2] = (tgrad[4 * ROWS : 5 * ROWS] + trec[2].astype(F32)).astype(BF16)
    for e in (1, 3):
        xfar(tsx, trx, 8, e).start()
    outer_send(1, 1)
    inner_sum(*ORDER[5])
    outer_send(1, 3)
    near_sends(*ORDER[7])
    for d in (1, 3):
        h = d // 2 * HALF
        sib(tsib, trec, 0, d).wait_recv()
        share = tgrad[2 * d * ROWS : (2 * d + 1) * ROWS] + trec[d].astype(F32)
        tgrad[2 * d * ROWS : (2 * d + 1) * ROWS] = share
        tsx[d] = share.astype(BF16)
        xfar(tsx, trx, 8, d).wait_recv()
        tsx[d, h : h + HALF] = (
            tgrad[2 * d * ROWS + h : 2 * d * ROWS + h + HALF] + trx[0, h : h + HALF].astype(F32)
        ).astype(BF16)
        xnear(tsx, trx, 8, d).start()
    inner_sum(*ORDER[6])
    outer_send(0, 3)
    cache_result()
    inner_sum(*ORDER[7])
    for h in (1, 0):
        for d in (1, 3):
            unear(h, d).wait_recv()
        ig_out[h * HALF : h * HALF + HALF] = part[SLAB[h, 0], 0] + uh[h, 1].astype(F32) + uh[h, 3].astype(F32)
    sib(tsib, trec, 0, 0).wait_recv()
    for d in (1, 3):
        xnear(tsx, trx, 8, d).wait_recv()
    tg_out[...] = tgrad[0:ROWS] + trec[0].astype(F32) + trx[1].astype(F32) + trx[3].astype(F32)

    for d in (1, 3):
        for h in (0, 1):
            go_out(h, d).wait_send()
            go_out_q(h, d).wait_send()
            for o in range(4):
                go_in(h, o, d).wait_send()
                go_in_q(h, o, d).wait_send()
                far(h, o, d).wait_send()
                near(h, o, d).wait_send()
            ufar(h, d).wait_send()
            unear(h, d).wait_send()
        for ref, ss, sr in ((txt, t_s, t_r), (cac, c_s, c_r)):
            along_x(ref, ss, sr, d).wait_send()
            half_x(ref, ss, sr, d).wait_send()
        for buf, rec, base in ((tsx, trx, 8), (csx, crx, 16)):
            xfar(buf, rec, base, d).wait_send()
            xnear(buf, rec, base, d).wait_send()
    for dz, dy in plane:
        tbl_to(dz, dy).wait_send()
    for d in range(4):
        to_sib(txt, t_s, t_r, d).wait_send()
        to_sib(cac, c_s, c_r, d).wait_send()
        sib(tsib, trec, 0, d).wait_send()
        sib(csib, crec, 4, d).wait_send()


def place_out(a, b, c, a_out, b_out, c_out, held, sems):
    ways = tuple(enumerate(((a, a_out), (b, b_out), (c, c_out))))
    into = [pltpu.make_async_copy(s, held.at[n], sems.at[n]) for n, (s, _) in ways]
    out = [pltpu.make_async_copy(held.at[n], t, sems.at[3 + n]) for n, (_, t) in ways]
    for copy in into:
        copy.start()
    for first, then in zip(into, out):
        first.wait()
        then.start()
    for copy in out:
        copy.wait()


def shards(images, texts, cache, mate_owner, mate_row, mate_count, log_scale, bias):
    vm = pl.BlockSpec(memory_space=pltpu.VMEM)
    dma = pltpu.SemaphoreType.DMA
    out = jax.ShapeDtypeStruct((ROWS, D), F32)
    four = lambda rows: pltpu.VMEM((4, rows, D), BF16)
    grads = (
        pl.pallas_call(
            kernel,
            out_shape=(out, out, out),
            in_specs=[vm] * 8,
            out_specs=(vm, vm, vm),
            scratch_shapes=[
                pltpu.VMEM((8, 4, HALF, D), BF16),
                pltpu.VMEM((8 * ROWS, D), BF16),
                pltpu.VMEM((8 * ROWS, D), BF16),
                pltpu.VMEM((8, ROWS, D), BF16),
                pltpu.VMEM((4, 4, 16, ROWS), I32),
                pltpu.VMEM((2 * ROWS, 8 * ROWS), BF16),
                pltpu.VMEM((8 * ROWS, D), F32),
                pltpu.VMEM((8, 4, HALF, D), F32),
                pltpu.VMEM((8, 4, HALF, D), BF16),
                pltpu.VMEM((8, 2, ROWS, D), BF16),
                pltpu.VMEM((2, 2, 4, QTR, D), BF16),
                pltpu.VMEM((2, 2, 4, HALF, D), BF16),
                pltpu.VMEM((2, 4, HALF, D), BF16),
                pltpu.VMEM((2, HALF, D), BF16),
                pltpu.VMEM((2, 4, HALF, D), BF16),
                four(ROWS), four(ROWS), four(ROWS), four(ROWS),
                four(ROWS), four(ROWS), four(ROWS), four(ROWS),
                pltpu.VMEM((4, ROWS, D), F32),
                dma((2, 4, 4)), dma((2, 4, 4)), dma((2, 2, 5)), dma((2, 2, 5)),
                dma((12,)), dma((12,)), dma((12,)), dma((12,)),
                dma((4, 4)), dma((4, 4)),
                dma((2, 2, 4)), dma((2, 2, 4)), dma((2, 2, 4)), dma((2, 2, 4)),
                dma((2, 8)), dma((2, 8)), dma((24,)), dma((24,)),
            ],
            compiler_params=pltpu.CompilerParams(
                collective_id=0, has_side_effects=True, vmem_limit_bytes=62 << 20
            ),
            cost_estimate=pl.CostEstimate(flops=17_000_000_000, bytes_accessed=4_000_000, transcendentals=2_000_000),
        )(
            log_scale.reshape(1, 1), bias.reshape(1, 1), images, texts, cache,
            mate_owner.T, mate_row.T, mate_count.reshape(1, ROWS),
        )
    )
    anywhere = pl.BlockSpec(memory_space=pl.ANY)
    return tuple(
        pl.pallas_call(
            place_out,
            out_shape=(out, out, out),
            in_specs=[anywhere] * 3,
            out_specs=(anywhere,) * 3,
            scratch_shapes=[pltpu.VMEM((3, ROWS, D), F32), dma((6,))],
        )(*grads)
    )


def solution(mesh):
    rows = P(("blk", "img"), None)
    return jax.shard_map(
        shards,
        mesh=mesh,
        in_specs=(rows, rows, rows, rows, rows, P(("blk", "img")), P(), P()),
        out_specs=(rows, rows, rows),
        check_vma=False,
    )
```

```python
import jax
import jax.numpy as jnp
from jax import lax
from jax.experimental import pallas as pl
from jax.experimental.pallas import tpu as pltpu
from jax.sharding import PartitionSpec as P

MESH = pl.DeviceIdType.MESH
F32, BF16, I32 = jnp.float32, jnp.bfloat16, jnp.int32
NT = (((1,), (1,)), ((), ()))
NN = (((1,), (0,)), ((), ()))
TN = (((0,), (0,)), ((), ()))
ROWS, D, HALF, QTR = 128, 1152, 64, 32
ORDER = ((1, 0), (1, 1), (0, 1), (1, 3), (0, 2), (1, 2), (0, 3), (0, 0))
SLAB = {key: n for n, key in enumerate(ORDER)}


def mm(a, b, dims):
    return lax.dot_general(a, b, dims, preferred_element_type=F32)


def kernel(
    ls_ref, bias_ref, images, texts, cache, owner, row, count,
    ig_out, tg_out, cg_out,
    img, txt, cac, gat, tbl, coeff, tgrad, part, pbf, sgr,
    rq, rh, usend, uq, uh, tsib, trec, csib, crec, tsx, trx, csx, crx, cgrad,
    h_s, h_r, q_s, q_r, t_s, t_r, c_s, c_r, k_s, k_r,
    rq_s, rq_r, rh_s, rh_r, u_s, u_r, x_s, x_r,
):
    blk, im = lax.axis_index("blk"), lax.axis_index("img")
    z, y, x, c = blk // 8, (blk // 2) % 4, (blk % 2) * 2 + im // 2, im % 2

    def dev(dz=0, dy=0, dx=0, dc=0):
        zz, yy, xx = (z + dz + 4) % 4, (y + dy + 4) % 4, (x + dx + 4) % 4
        return ((zz * 4 + yy) * 2 + xx // 2, (xx % 2) * 2 + (c + dc) % 2)

    def rc(src, dst, ss, rs, to):
        return pltpu.make_async_remote_copy(
            src_ref=src, dst_ref=dst, send_sem=ss, recv_sem=rs, device_id=to, device_id_type=MESH
        )

    def outer_dev(h, d):
        return dev(d) if h else dev(0, d)

    def inner_dev(h, d):
        return dev(0, d) if h else dev(d)

    def quarter(d):
        return pl.ds(d // 2 * QTR, QTR)

    def go_out(h, d):
        return rc(img.at[SLAB[h, 0], 0], img.at[SLAB[h, d], 0], h_s.at[h, d, 0], h_r.at[h, d, 0], outer_dev(h, -d))

    def go_out_q(h, d):
        q = quarter(d)
        return rc(img.at[SLAB[h, d], 0, q], img.at[SLAB[h, 2], 0, q],
                  q_s.at[h, d // 2, 4], q_r.at[h, d // 2, 4], outer_dev(h, -d))

    def go_in(h, o, d):
        return rc(img.at[SLAB[h, o], 0], img.at[SLAB[h, o], d], h_s.at[h, o, d], h_r.at[h, o, d], inner_dev(h, -d))

    def go_in_q(h, o, d):
        q = quarter(d)
        return rc(img.at[SLAB[h, o], d, q], img.at[SLAB[h, o], 2, q],
                  q_s.at[h, d // 2, o], q_r.at[h, d // 2, o], inner_dev(h, -d))

    def rows_of(ref, n):
        return ref.at[pl.ds(n * ROWS, ROWS)]

    def along_x(ref, sems, semr, d):
        return rc(rows_of(ref, 0), rows_of(ref, 2 * d), sems.at[2 * d], semr.at[2 * d], dev(dx=-d))

    def half_x(ref, sems, semr, d):
        h = d // 2 * HALF
        return rc(ref.at[pl.ds(2 * d * ROWS + h, HALF)], ref.at[pl.ds(4 * ROWS + h, HALF)],
                  sems.at[8 + d], semr.at[8 + d], dev(dx=-d))

    def to_sib(ref, sems, semr, d):
        return rc(rows_of(ref, 2 * d), rows_of(ref, 2 * d + 1), sems.at[2 * d + 1], semr.at[2 * d + 1], dev(dc=1))

    def tbl_to(dz, dy):
        return rc(tbl.at[0, 0], tbl.at[dz, dy], k_s.at[dz, dy], k_r.at[dz, dy], dev(-dz, -dy))

    plane = [(dz, dy) for dz in range(4) for dy in range(4) if dz or dy]
    peers = [dev(dz, dy) for dz, dy in plane] + [dev(dx=1), dev(dx=3), dev(dc=1)]
    barrier = pltpu.get_barrier_semaphore()
    for to in peers:
        pl.semaphore_signal(barrier, inc=1, device_id=to, device_id_type=MESH)
    for h in (0, 1):
        img[SLAB[h, 0], 0] = images[h * HALF : h * HALF + HALF]
    txt[0:ROWS] = texts[...]
    cac[0:ROWS] = cache[...]
    lane = lax.broadcasted_iota(I32, (ROWS, ROWS), 1)
    sub = lax.broadcasted_iota(I32, (ROWS, ROWS), 0)
    below = (sub > lane).astype(BF16)

    def down(line):
        return jnp.transpose(jnp.broadcast_to(line.astype(F32), (ROWS, ROWS)))

    live = down(count[...])
    carry = jnp.zeros((1, ROWS), F32)
    picked_r = [jnp.zeros((1, ROWS), F32) for _ in range(8)]
    picked_c = [jnp.zeros((1, ROWS), F32) for _ in range(8)]
    row1 = (sub + 1).astype(F32)
    for k in range(4):
        hits = ((down(owner[k : k + 1, :]) == lane.astype(F32)) & (live > k)).astype(F32)
        rank = mm(below, hits.astype(BF16), NN) + carry
        carry = carry + jnp.sum(hits, axis=0, keepdims=True)
        cols = down(row[k : k + 1, :])
        for s in range(8):
            sel = jnp.where(rank == s, hits, 0.0)
            picked_r[s] = picked_r[s] + jnp.sum(sel * row1, axis=0, keepdims=True)
            picked_c[s] = picked_c[s] + jnp.sum(sel * cols, axis=0, keepdims=True)
    for s in range(8):
        tbl[0, 0, s : s + 1, :] = picked_r[s].astype(I32)
        tbl[0, 0, 8 + s : 9 + s, :] = picked_c[s].astype(I32)
    pl.semaphore_wait(barrier, len(peers))
    for dz, dy in plane:
        tbl_to(dz, dy).start()

    for d in (1, 3):
        for h in (0, 1):
            go_out(h, d).start()
        along_x(txt, t_s, t_r, d).start()
    to_sib(txt, t_s, t_r, 0).start()
    for d in (1, 3):
        for h in (0, 1):
            go_in(h, 0, d).start()

    for d in (1, 3):
        for h in (0, 1):
            go_out(h, d).wait_recv()
            go_out_q(h, d).start()
            for e in (1, 3):
                go_in(h, d, e).start()
    for d in (1, 3):
        for h in (0, 1):
            go_in(h, 0, d).wait_recv()
            go_in_q(h, 0, d).start()
    for d in (1, 3):
        along_x(txt, t_s, t_r, d).wait_recv()
        half_x(txt, t_s, t_r, d).start()
        to_sib(txt, t_s, t_r, d).start()
    for d in (1, 3):
        along_x(cac, c_s, c_r, d).start()
    to_sib(cac, c_s, c_r, 0).start()
    for h in (0, 1):
        for d in (1, 3):
            go_out_q(h, d).wait_recv()
        for d in (1, 3):
            go_in(h, 2, d).start()
    tgrad[...] = jnp.zeros_like(tgrad)
    part[...] = jnp.zeros_like(part)
    for dz, dy in plane:
        tbl_to(dz, dy).wait_recv()
    for o in (1, 3):
        for h in (0, 1):
            for d in (1, 3):
                go_in(h, o, d).wait_recv()
                go_in_q(h, o, d).start()
    for d in (1, 3):
        half_x(txt, t_s, t_r, d).wait_recv()
    to_sib(txt, t_s, t_r, 2).start()

    scale = jnp.exp(ls_ref[...])
    half = 0.5 * scale
    shift = 0.5 * bias_ref[...]

    def text_step(t):
        mine = img[t].reshape(2 * ROWS, D)
        logit = mm(mine, txt[...], NT)
        coeff[...] = (half + half * jnp.tanh(half * logit + shift)).astype(BF16)

        for h in (0, 1):
            @pl.when(t == SLAB[h, 0])
            def _():
                own = mm(img[SLAB[h, 0], 0], txt[0:ROWS], NT)
                prob = half + half * jnp.tanh(half * own + shift)
                same = sub[0:HALF] + h * HALF == lane[0:HALF]
                coeff[0:HALF, 0:ROWS] = (prob - jnp.where(same, scale, 0.0)).astype(BF16)

        co = coeff[...]
        total = part[t] + mm(co, txt[...], NN).reshape(4, HALF, D)
        part[t] = total
        pbf[t] = total.astype(BF16)
        tgrad[...] += mm(co, mine, TN)

    def spread_lanes(table, first):
        want = lax.broadcasted_iota(I32, (ROWS, ROWS), 0)
        b = lax.broadcasted_iota(I32, (ROWS, ROWS), 1) // 16
        of = first + ((x + b // 2) % 4) * 2 + (c + b) % 2
        return mm(table, (want == of).astype(BF16), NN)

    first = (z * 4 + y) * 8
    tab = tbl[...].reshape(16, 2, 8, ROWS)
    tab_r = tab[:, 0].reshape(ROWS, ROWS).astype(F32).astype(BF16)
    tab_c = tab[:, 1].reshape(ROWS, ROWS).astype(F32).astype(BF16)

    def column(b):
        of = first + ((x + b // 2) % 4) * 2 + (c + b) % 2
        want = lax.broadcasted_iota(I32, (ROWS, ROWS), 0)
        return (mm(tab_c, (want == of).astype(BF16), NN) == lane.astype(F32)).astype(BF16)

    lanes_r = spread_lanes(tab_r, first)

    def gather_rows():
        for d in range(4):
            to_sib(cac, c_s, c_r, d).wait_recv()
        for b in range(8):
            gat[b] = mm(column(b), cac[pl.ds(b * ROWS, ROWS)], NN).astype(BF16)

    def far(h, o, d):
        return rc(pbf.at[SLAB[h, o], 2, quarter(d)], rq.at[h, d // 2, o],
                  rq_s.at[h, d // 2, o], rq_r.at[h, d // 2, o], inner_dev(h, d))

    def near(h, o, d):
        return rc(pbf.at[SLAB[h, o], d], rh.at[h, d // 2, o],
                  rh_s.at[h, d // 2, o], rh_r.at[h, d // 2, o], inner_dev(h, d))

    def ufar(h, d):
        return rc(usend.at[h, 2, quarter(d)], uq.at[h, quarter(d)], u_s.at[h, d], u_r.at[h, d], outer_dev(h, d))

    def unear(h, d):
        return rc(usend.at[h, d], uh.at[h, d], u_s.at[h, 4 + d], u_r.at[h, 4 + d], outer_dev(h, d))

    def far_sends(h, o):
        for d in (1, 3):
            far(h, o, d).start()

    def near_sends(h, o):
        n = SLAB[h, o]
        for d in (1, 3):
            far(h, o, d).wait_recv()
            q = d // 2 * QTR
            pbf[n, d, q : q + QTR] = (part[n, d, q : q + QTR] + rq[h, d // 2, o].astype(F32)).astype(BF16)
            near(h, o, d).start()

    def inner_sum(h, o):
        n = SLAB[h, o]
        for d in (1, 3):
            near(h, o, d).wait_recv()
        total = part[n, 0] + rh[h, 0, o].astype(F32) + rh[h, 1, o].astype(F32)
        if o == 2:
            usend[h, 2] = total.astype(BF16)
            for d in (1, 3):
                ufar(h, d).start()
        else:
            part[n, 0] = total

    def outer_send(h, o):
        n, q = SLAB[h, o], o // 2 * QTR
        ufar(h, o).wait_recv()
        usend[h, o] = part[n, 0].astype(BF16)
        usend[h, o, q : q + QTR] = (part[n, 0, q : q + QTR] + uq[h, q : q + QTR].astype(F32)).astype(BF16)
        unear(h, o).start()

    def mate_step(dz, p):
        pair = dz * 2 + p
        mine = jnp.concatenate(
            [img[SLAB[0, 2 * p], dz], img[SLAB[0, 2 * p + 1], dz], img[SLAB[1, dz], 2 * p], img[SLAB[1, dz], 2 * p + 1]],
            axis=0,
        )
        emb = gat[:, pair * 16 : pair * 16 + 16, :].reshape(ROWS, D)
        keep = jnp.where(sub == pair * 16 + lane % 16, lanes_r, 0.0)
        at_row = jnp.sum(keep, axis=0, keepdims=True)
        big_sub = lax.broadcasted_iota(I32, (2 * ROWS, ROWS), 0)
        second = lax.broadcasted_iota(I32, (1, ROWS), 1) % 16 // 8
        moved = jnp.where(at_row > HALF + 0.5, 64.0, 0.0) + second.astype(F32) * HALF
        target = jnp.where(at_row > 0.5, at_row - 1.0 + moved, -1.0)
        named = big_sub.astype(F32) == target
        logit = mm(mine, emb, NT)
        wt = jnp.where(named, half * jnp.tanh(half * logit + shift) - half, 0.0).astype(BF16)
        grad = mm(wt, emb, NN)
        part[SLAB[0, 2 * p], dz] += grad[0:HALF]
        part[SLAB[0, 2 * p + 1], dz] += grad[HALF:ROWS]
        part[SLAB[1, dz], 2 * p] += grad[ROWS : ROWS + HALF]
        part[SLAB[1, dz], 2 * p + 1] += grad[ROWS + HALF :]
        slots = mm(wt, mine, TN)
        top = slots.astype(BF16)
        sgr[:, 0, pair * 16 : pair * 16 + 16, :] = top.reshape(8, 16, D)
        sgr[:, 1, pair * 16 : pair * 16 + 16, :] = (slots - top.astype(F32)).astype(BF16).reshape(8, 16, D)
    def in_quarters(h, o):
        for d in (1, 3):
            go_in_q(h, o, d).wait_recv()

    def edges():
        for h in (0, 1):
            for d in (1, 3):
                go_in(h, 2, d).wait_recv()
                go_in_q(h, 2, d).start()

    def cache_near():
        for d in (1, 3):
            along_x(cac, c_s, c_r, d).wait_recv()
            half_x(cac, c_s, c_r, d).start()
            to_sib(cac, c_s, c_r, d).start()

    def cache_far():
        for d in (1, 3):
            half_x(cac, c_s, c_r, d).wait_recv()
        to_sib(cac, c_s, c_r, 2).start()

    def send_slab(h, o):
        n = SLAB[h, o]
        pbf[n] = part[n].astype(BF16)
        far_sends(h, o)

    for d in range(4):
        to_sib(txt, t_s, t_r, d).wait_recv()

    def sib(buf, rec, base, d):
        return rc(buf.at[d], rec.at[d], x_s.at[base + d], x_r.at[base + d], dev(dc=1))

    def xfar(buf, rec, base, d):
        h = pl.ds(d // 2 * HALF, HALF)
        return rc(buf.at[2, h], rec.at[0, h], x_s.at[base + d], x_r.at[base + d], dev(dx=d))

    def xnear(buf, rec, base, d):
        return rc(buf.at[d], rec.at[d], x_s.at[base + 3 + d], x_r.at[base + 3 + d], dev(dx=d))

    def owner_grad(b):
        spots = column(b)
        both = jnp.concatenate([spots, spots], axis=0)
        return mm(both, sgr[b].reshape(2 * ROWS, D), TN)

    def cache_to_sibling():
        for d in (2, 1, 3, 0):
            csib[d] = owner_grad(2 * d + 1).astype(BF16)
            sib(csib, crec, 4, d).start()

    def cache_far_sends():
        for d in (2, 1, 3, 0):
            cgrad[d] = owner_grad(2 * d)
            sib(csib, crec, 4, d).wait_recv()
            cgrad[d] += crec[d].astype(F32)
            if d == 2:
                csx[2] = cgrad[2].astype(BF16)
                for e in (1, 3):
                    xfar(csx, crx, 16, e).start()

    def cache_near_sends():
        for d in (1, 3):
            xfar(csx, crx, 16, d).wait_recv()
            h = d // 2 * HALF
            csx[d] = cgrad[d].astype(BF16)
            csx[d, h : h + HALF] = (cgrad[d, h : h + HALF] + crx[0, h : h + HALF].astype(F32)).astype(BF16)
            xnear(csx, crx, 16, d).start()

    def cache_result():
        for d in (1, 3):
            xnear(csx, crx, 16, d).wait_recv()
        cg_out[...] = cgrad[0] + crx[1].astype(F32) + crx[3].astype(F32)

    def step(t, carried):
        @pl.when(t == 0)
        def _():
            in_quarters(1, 0)

        @pl.when(t == 1)
        def _():
            edges()
            cache_near()
            in_quarters(1, 1)

        @pl.when(t == 2)
        def _():
            in_quarters(0, 1)

        @pl.when(t == 3)
        def _():
            cache_far()
            in_quarters(1, 3)

        @pl.when(t == 4)
        def _():
            gather_rows()
            mate_step(0, 0)
            mate_step(0, 1)
            send_slab(1, 0)
            mate_step(1, 0)
            mate_step(1, 1)
            send_slab(1, 1)
            mate_step(3, 0)
            in_quarters(0, 0)
            mate_step(2, 0)
            send_slab(0, 1)
            mate_step(3, 1)
            send_slab(1, 3)
            near_sends(1, 0)
            in_quarters(0, 2)
            in_quarters(0, 3)
            in_quarters(1, 2)
            mate_step(2, 1)
            cache_to_sibling()
            near_sends(1, 1)

        text_step(t)
        after = {4: ((0, 1), (1, 3)), 5: ((0, 2),), 6: ((1, 2),), 7: ((0, 3),)}
        for n in range(4, 8):
            @pl.when(t == n)
            def _():
                far_sends(*ORDER[n])
                for key in after[n]:
                    near_sends(*key)
                if n == 4:
                    cache_far_sends()
                if n == 5:
                    cache_near_sends()

        return carried

    lax.fori_loop(0, 8, step, 0)

    for d in (2, 1, 3, 0):
        tsib[d] = tgrad[(2 * d + 1) * ROWS : (2 * d + 2) * ROWS].astype(BF16)
        sib(tsib, trec, 0, d).start()
    sib(tsib, trec, 0, 2).wait_recv()
    tsx[2] = (tgrad[4 * ROWS : 5 * ROWS] + trec[2].astype(F32)).astype(BF16)
    for e in (1, 3):
        xfar(tsx, trx, 8, e).start()
    inner_sum(0, 2)
    near_sends(0, 0)
    inner_sum(1, 2)
    for d in (1, 3):
        h = d // 2 * HALF
        sib(tsib, trec, 0, d).wait_recv()
        share = tgrad[2 * d * ROWS : (2 * d + 1) * ROWS] + trec[d].astype(F32)
        xfar(tsx, trx, 8, d).wait_recv()
        tsx[d] = share.astype(BF16)
        tsx[d, h : h + HALF] = (share[h : h + HALF] + trx[0, h : h + HALF].astype(F32)).astype(BF16)
        xnear(tsx, trx, 8, d).start()
    inner_sum(0, 1)
    outer_send(0, 1)
    inner_sum(1, 1)
    outer_send(1, 1)
    inner_sum(1, 3)
    outer_send(1, 3)
    inner_sum(0, 3)
    outer_send(0, 3)
    inner_sum(1, 0)
    cache_result()
    inner_sum(0, 0)
    for h in (1, 0):
        for d in (1, 3):
            unear(h, d).wait_recv()
        ig_out[h * HALF : h * HALF + HALF] = part[SLAB[h, 0], 0] + uh[h, 1].astype(F32) + uh[h, 3].astype(F32)
    sib(tsib, trec, 0, 0).wait_recv()
    for d in (1, 3):
        xnear(tsx, trx, 8, d).wait_recv()
    tg_out[...] = tgrad[0:ROWS] + trec[0].astype(F32) + trx[1].astype(F32) + trx[3].astype(F32)

    for d in (1, 3):
        for h in (0, 1):
            go_out(h, d).wait_send()
            go_out_q(h, d).wait_send()
            for o in range(4):
                go_in(h, o, d).wait_send()
                go_in_q(h, o, d).wait_send()
                far(h, o, d).wait_send()
                near(h, o, d).wait_send()
            ufar(h, d).wait_send()
            unear(h, d).wait_send()
        for ref, ss, sr in ((txt, t_s, t_r), (cac, c_s, c_r)):
            along_x(ref, ss, sr, d).wait_send()
            half_x(ref, ss, sr, d).wait_send()
        for buf, rec, base in ((tsx, trx, 8), (csx, crx, 16)):
            xfar(buf, rec, base, d).wait_send()
            xnear(buf, rec, base, d).wait_send()
    for dz, dy in plane:
        tbl_to(dz, dy).wait_send()
    for d in range(4):
        to_sib(txt, t_s, t_r, d).wait_send()
        to_sib(cac, c_s, c_r, d).wait_send()
        sib(tsib, trec, 0, d).wait_send()
        sib(csib, crec, 4, d).wait_send()


def place_out(a, b, c, a_out, b_out, c_out, held, sems):
    ways = tuple(enumerate(((a, a_out), (b, b_out), (c, c_out))))
    into = [pltpu.make_async_copy(s, held.at[n], sems.at[n]) for n, (s, _) in ways]
    out = [pltpu.make_async_copy(held.at[n], t, sems.at[3 + n]) for n, (_, t) in ways]
    for copy in into:
        copy.start()
    for first, then in zip(into, out):
        first.wait()
        then.start()
    for copy in out:
        copy.wait()


def shards(images, texts, cache, mate_owner, mate_row, mate_count, log_scale, bias):
    vm = pl.BlockSpec(memory_space=pltpu.VMEM)
    dma = pltpu.SemaphoreType.DMA
    out = jax.ShapeDtypeStruct((ROWS, D), F32)
    four = lambda rows: pltpu.VMEM((4, rows, D), BF16)
    grads = (
        pl.pallas_call(
            kernel,
            out_shape=(out, out, out),
            in_specs=[vm] * 8,
            out_specs=(vm, vm, vm),
            scratch_shapes=[
                pltpu.VMEM((8, 4, HALF, D), BF16),
                pltpu.VMEM((8 * ROWS, D), BF16),
                pltpu.VMEM((8 * ROWS, D), BF16),
                pltpu.VMEM((8, ROWS, D), BF16),
                pltpu.VMEM((4, 4, 16, ROWS), I32),
                pltpu.VMEM((2 * ROWS, 8 * ROWS), BF16),
                pltpu.VMEM((8 * ROWS, D), F32),
                pltpu.VMEM((8, 4, HALF, D), F32),
                pltpu.VMEM((8, 4, HALF, D), BF16),
                pltpu.VMEM((8, 2, ROWS, D), BF16),
                pltpu.VMEM((2, 2, 4, QTR, D), BF16),
                pltpu.VMEM((2, 2, 4, HALF, D), BF16),
                pltpu.VMEM((2, 4, HALF, D), BF16),
                pltpu.VMEM((2, HALF, D), BF16),
                pltpu.VMEM((2, 4, HALF, D), BF16),
                four(ROWS), four(ROWS), four(ROWS), four(ROWS),
                four(ROWS), four(ROWS), four(ROWS), four(ROWS),
                pltpu.VMEM((4, ROWS, D), F32),
                dma((2, 4, 4)), dma((2, 4, 4)), dma((2, 2, 5)), dma((2, 2, 5)),
                dma((12,)), dma((12,)), dma((12,)), dma((12,)),
                dma((4, 4)), dma((4, 4)),
                dma((2, 2, 4)), dma((2, 2, 4)), dma((2, 2, 4)), dma((2, 2, 4)),
                dma((2, 8)), dma((2, 8)), dma((24,)), dma((24,)),
            ],
            compiler_params=pltpu.CompilerParams(
                collective_id=0, has_side_effects=True, vmem_limit_bytes=62 << 20
            ),
            cost_estimate=pl.CostEstimate(flops=17_000_000_000, bytes_accessed=4_000_000, transcendentals=2_000_000),
        )(
            log_scale.reshape(1, 1), bias.reshape(1, 1), images, texts, cache,
            mate_owner.T, mate_row.T, mate_count.reshape(1, ROWS),
        )
    )
    anywhere = pl.BlockSpec(memory_space=pl.ANY)
    return tuple(
        pl.pallas_call(
            place_out,
            out_shape=(out, out, out),
            in_specs=[anywhere] * 3,
            out_specs=(anywhere,) * 3,
            scratch_shapes=[pltpu.VMEM((3, ROWS, D), F32), dma((6,))],
        )(*grads)
    )


def solution(mesh):
    rows = P(("blk", "img"), None)
    return jax.shard_map(
        shards,
        mesh=mesh,
        in_specs=(rows, rows, rows, rows, rows, P(("blk", "img")), P(), P()),
        out_specs=(rows, rows, rows),
        check_vma=False,
    )
```

```python
import jax
import jax.numpy as jnp
from jax import lax
from jax.experimental import pallas as pl
from jax.experimental.pallas import tpu as pltpu
from jax.sharding import PartitionSpec as P

MESH = pl.DeviceIdType.MESH
F32, BF16, I32 = jnp.float32, jnp.bfloat16, jnp.int32
NT = (((1,), (1,)), ((), ()))
NN = (((1,), (0,)), ((), ()))
TN = (((0,), (0,)), ((), ()))
ROWS, D, HALF, QTR = 128, 1152, 64, 32
ORDER = ((1, 0), (1, 1), (0, 1), (1, 3), (0, 2), (1, 2), (0, 3), (0, 0))
SLAB = {key: n for n, key in enumerate(ORDER)}


def mm(a, b, dims):
    return lax.dot_general(a, b, dims, preferred_element_type=F32)


def kernel(
    ls_ref, bias_ref, images, texts, cache, owner, row, count,
    ig_out, tg_out, cg_out,
    img, txt, cac, gat, tbl, coeff, tgrad, part, pbf, sgr,
    rq, rh, usend, uq, uh, tsib, trec, csib, crec, tsx, trx, csx, crx, cgrad, hot,
    h_s, h_r, q_s, q_r, t_s, t_r, c_s, c_r, k_s, k_r,
    rq_s, rq_r, rh_s, rh_r, u_s, u_r, x_s, x_r,
):
    blk, im = lax.axis_index("blk"), lax.axis_index("img")
    z, y, x, c = blk // 8, (blk // 2) % 4, (blk % 2) * 2 + im // 2, im % 2

    def dev(dz=0, dy=0, dx=0, dc=0):
        zz, yy, xx = (z + dz + 4) % 4, (y + dy + 4) % 4, (x + dx + 4) % 4
        return ((zz * 4 + yy) * 2 + xx // 2, (xx % 2) * 2 + (c + dc) % 2)

    def rc(src, dst, ss, rs, to):
        return pltpu.make_async_remote_copy(
            src_ref=src, dst_ref=dst, send_sem=ss, recv_sem=rs, device_id=to, device_id_type=MESH
        )

    def outer_dev(h, d):
        return dev(d) if h else dev(0, d)

    def inner_dev(h, d):
        return dev(0, d) if h else dev(d)

    def quarter(d):
        return pl.ds(d // 2 * QTR, QTR)

    def go_out(h, d):
        return rc(img.at[SLAB[h, 0], 0], img.at[SLAB[h, d], 0], h_s.at[h, d, 0], h_r.at[h, d, 0], outer_dev(h, -d))

    def go_out_q(h, d):
        q = quarter(d)
        return rc(img.at[SLAB[h, d], 0, q], img.at[SLAB[h, 2], 0, q],
                  q_s.at[h, d // 2, 4], q_r.at[h, d // 2, 4], outer_dev(h, -d))

    def go_in(h, o, d):
        return rc(img.at[SLAB[h, o], 0], img.at[SLAB[h, o], d], h_s.at[h, o, d], h_r.at[h, o, d], inner_dev(h, -d))

    def go_in_q(h, o, d):
        q = quarter(d)
        return rc(img.at[SLAB[h, o], d, q], img.at[SLAB[h, o], 2, q],
                  q_s.at[h, d // 2, o], q_r.at[h, d // 2, o], inner_dev(h, -d))

    def rows_of(ref, n):
        return ref.at[pl.ds(n * ROWS, ROWS)]

    def along_x(ref, sems, semr, d):
        return rc(rows_of(ref, 0), rows_of(ref, 2 * d), sems.at[2 * d], semr.at[2 * d], dev(dx=-d))

    def half_x(ref, sems, semr, d):
        h = d // 2 * HALF
        return rc(ref.at[pl.ds(2 * d * ROWS + h, HALF)], ref.at[pl.ds(4 * ROWS + h, HALF)],
                  sems.at[8 + d], semr.at[8 + d], dev(dx=-d))

    def to_sib(ref, sems, semr, d):
        return rc(rows_of(ref, 2 * d), rows_of(ref, 2 * d + 1), sems.at[2 * d + 1], semr.at[2 * d + 1], dev(dc=1))

    def tbl_to(dz, dy):
        return rc(tbl.at[0, 0], tbl.at[dz, dy], k_s.at[dz, dy], k_r.at[dz, dy], dev(-dz, -dy))

    plane = [(dz, dy) for dz in range(4) for dy in range(4) if dz or dy]
    peers = [dev(dz, dy) for dz, dy in plane] + [dev(dx=1), dev(dx=3), dev(dc=1)]
    barrier = pltpu.get_barrier_semaphore()
    for to in peers:
        pl.semaphore_signal(barrier, inc=1, device_id=to, device_id_type=MESH)
    for h in (0, 1):
        img[SLAB[h, 0], 0] = images[h * HALF : h * HALF + HALF]
    txt[0:ROWS] = texts[...]
    cac[0:ROWS] = cache[...]
    lane = lax.broadcasted_iota(I32, (ROWS, ROWS), 1)
    sub = lax.broadcasted_iota(I32, (ROWS, ROWS), 0)
    below = (sub > lane).astype(BF16)

    def down(line):
        return jnp.transpose(jnp.broadcast_to(line.astype(F32), (ROWS, ROWS)))

    live = down(count[...])
    carry = jnp.zeros((1, ROWS), F32)
    picked_r = [jnp.zeros((1, ROWS), F32) for _ in range(8)]
    picked_c = [jnp.zeros((1, ROWS), F32) for _ in range(8)]
    row1 = (sub + 1).astype(F32)
    for k in range(4):
        hits = ((down(owner[k : k + 1, :]) == lane.astype(F32)) & (live > k)).astype(F32)
        rank = mm(below, hits.astype(BF16), NN) + carry
        carry = carry + jnp.sum(hits, axis=0, keepdims=True)
        cols = down(row[k : k + 1, :])
        for s in range(8):
            sel = jnp.where(rank == s, hits, 0.0)
            picked_r[s] = picked_r[s] + jnp.sum(sel * row1, axis=0, keepdims=True)
            picked_c[s] = picked_c[s] + jnp.sum(sel * cols, axis=0, keepdims=True)
    for s in range(8):
        tbl[0, 0, s : s + 1, :] = picked_r[s].astype(I32)
        tbl[0, 0, 8 + s : 9 + s, :] = picked_c[s].astype(I32)
    pl.semaphore_wait(barrier, len(peers))
    for dz, dy in plane:
        tbl_to(dz, dy).start()

    for d in (1, 3):
        for h in (0, 1):
            go_out(h, d).start()
        along_x(txt, t_s, t_r, d).start()
    to_sib(txt, t_s, t_r, 0).start()
    for d in (1, 3):
        for h in (0, 1):
            go_in(h, 0, d).start()

    for d in (1, 3):
        for h in (0, 1):
            go_out(h, d).wait_recv()
            go_out_q(h, d).start()
            for e in (1, 3):
                go_in(h, d, e).start()
    for d in (1, 3):
        for h in (0, 1):
            go_in(h, 0, d).wait_recv()
            go_in_q(h, 0, d).start()
    for d in (1, 3):
        along_x(txt, t_s, t_r, d).wait_recv()
        half_x(txt, t_s, t_r, d).start()
        to_sib(txt, t_s, t_r, d).start()
    for d in (1, 3):
        along_x(cac, c_s, c_r, d).start()
    to_sib(cac, c_s, c_r, 0).start()
    for h in (0, 1):
        for d in (1, 3):
            go_out_q(h, d).wait_recv()
        for d in (1, 3):
            go_in(h, 2, d).start()
    tgrad[...] = jnp.zeros_like(tgrad)
    part[...] = jnp.zeros_like(part)
    for dz, dy in plane:
        tbl_to(dz, dy).wait_recv()
    for o in (1, 3):
        for h in (0, 1):
            for d in (1, 3):
                go_in(h, o, d).wait_recv()
                go_in_q(h, o, d).start()
    for d in (1, 3):
        half_x(txt, t_s, t_r, d).wait_recv()
    to_sib(txt, t_s, t_r, 2).start()

    scale = jnp.exp(ls_ref[...])
    half = 0.5 * scale
    shift = 0.5 * bias_ref[...]

    def text_step(t):
        mine = img[t].reshape(2 * ROWS, D)
        logit = mm(mine, txt[...], NT)
        coeff[...] = (half + half * jnp.tanh(half * logit + shift)).astype(BF16)

        for h in (0, 1):
            @pl.when(t == SLAB[h, 0])
            def _():
                own = mm(img[SLAB[h, 0], 0], txt[0:ROWS], NT)
                prob = half + half * jnp.tanh(half * own + shift)
                same = sub[0:HALF] + h * HALF == lane[0:HALF]
                coeff[0:HALF, 0:ROWS] = (prob - jnp.where(same, scale, 0.0)).astype(BF16)

        co = coeff[...]
        total = part[t] + mm(co, txt[...], NN).reshape(4, HALF, D)
        part[t] = total
        pbf[t] = total.astype(BF16)
        tgrad[...] += mm(co, mine, TN)

    def spread_lanes(table, first):
        want = lax.broadcasted_iota(I32, (ROWS, ROWS), 0)
        b = lax.broadcasted_iota(I32, (ROWS, ROWS), 1) // 16
        of = first + ((x + b // 2) % 4) * 2 + (c + b) % 2
        return mm(table, (want == of).astype(BF16), NN)

    first = (z * 4 + y) * 8
    tab = tbl[...].reshape(16, 2, 8, ROWS)
    tab_r = tab[:, 0].reshape(ROWS, ROWS).astype(F32).astype(BF16)
    tab_c = tab[:, 1].reshape(ROWS, ROWS).astype(F32).astype(BF16)

    def column(b):
        of = first + ((x + b // 2) % 4) * 2 + (c + b) % 2
        want = lax.broadcasted_iota(I32, (ROWS, ROWS), 0)
        return (mm(tab_c, (want == of).astype(BF16), NN) == lane.astype(F32)).astype(BF16)

    lanes_r = spread_lanes(tab_r, first)

    def gather_rows():
        for d in range(4):
            to_sib(cac, c_s, c_r, d).wait_recv()
        for b in range(8):
            hot[b] = column(b)
            gat[b] = mm(hot[b], cac[pl.ds(b * ROWS, ROWS)], NN).astype(BF16)

    def far(h, o, d):
        return rc(pbf.at[SLAB[h, o], 2, quarter(d)], rq.at[h, d // 2, o],
                  rq_s.at[h, d // 2, o], rq_r.at[h, d // 2, o], inner_dev(h, d))

    def near(h, o, d):
        return rc(pbf.at[SLAB[h, o], d], rh.at[h, d // 2, o],
                  rh_s.at[h, d // 2, o], rh_r.at[h, d // 2, o], inner_dev(h, d))

    def ufar(h, d):
        return rc(usend.at[h, 2, quarter(d)], uq.at[h, quarter(d)], u_s.at[h, d], u_r.at[h, d], outer_dev(h, d))

    def unear(h, d):
        return rc(usend.at[h, d], uh.at[h, d], u_s.at[h, 4 + d], u_r.at[h, 4 + d], outer_dev(h, d))

    def far_sends(h, o):
        for d in (1, 3):
            far(h, o, d).start()

    def near_sends(h, o):
        n = SLAB[h, o]
        for d in (1, 3):
            far(h, o, d).wait_recv()
            q = d // 2 * QTR
            pbf[n, d, q : q + QTR] = (part[n, d, q : q + QTR] + rq[h, d // 2, o].astype(F32)).astype(BF16)
            near(h, o, d).start()

    def inner_sum(h, o):
        n = SLAB[h, o]
        for d in (1, 3):
            near(h, o, d).wait_recv()
        total = part[n, 0] + rh[h, 0, o].astype(F32) + rh[h, 1, o].astype(F32)
        if o == 2:
            usend[h, 2] = total.astype(BF16)
            for d in (1, 3):
                ufar(h, d).start()
        else:
            part[n, 0] = total

    def outer_send(h, o):
        n, q = SLAB[h, o], o // 2 * QTR
        ufar(h, o).wait_recv()
        usend[h, o] = part[n, 0].astype(BF16)
        usend[h, o, q : q + QTR] = (part[n, 0, q : q + QTR] + uq[h, q : q + QTR].astype(F32)).astype(BF16)
        unear(h, o).start()

    def mate_step(dz, p):
        pair = dz * 2 + p
        mine = jnp.concatenate(
            [img[SLAB[0, 2 * p], dz], img[SLAB[0, 2 * p + 1], dz], img[SLAB[1, dz], 2 * p], img[SLAB[1, dz], 2 * p + 1]],
            axis=0,
        )
        emb = gat[:, pair * 16 : pair * 16 + 16, :].reshape(ROWS, D)
        keep = jnp.where(sub == pair * 16 + lane % 16, lanes_r, 0.0)
        at_row = jnp.sum(keep, axis=0, keepdims=True)
        big_sub = lax.broadcasted_iota(I32, (2 * ROWS, ROWS), 0)
        second = lax.broadcasted_iota(I32, (1, ROWS), 1) % 16 // 8
        moved = jnp.where(at_row > HALF + 0.5, 64.0, 0.0) + second.astype(F32) * HALF
        target = jnp.where(at_row > 0.5, at_row - 1.0 + moved, -1.0)
        named = big_sub.astype(F32) == target
        logit = mm(mine, emb, NT)
        wt = jnp.where(named, half * jnp.tanh(half * logit + shift) - half, 0.0).astype(BF16)
        grad = mm(wt, emb, NN)
        part[SLAB[0, 2 * p], dz] += grad[0:HALF]
        part[SLAB[0, 2 * p + 1], dz] += grad[HALF:ROWS]
        part[SLAB[1, dz], 2 * p] += grad[ROWS : ROWS + HALF]
        part[SLAB[1, dz], 2 * p + 1] += grad[ROWS + HALF :]
        slots = mm(wt, mine, TN)
        top = slots.astype(BF16)
        sgr[:, 0, pair * 16 : pair * 16 + 16, :] = top.reshape(8, 16, D)
        sgr[:, 1, pair * 16 : pair * 16 + 16, :] = (slots - top.astype(F32)).astype(BF16).reshape(8, 16, D)
    def in_quarters(h, o):
        for d in (1, 3):
            go_in_q(h, o, d).wait_recv()

    def edges():
        for h in (0, 1):
            for d in (1, 3):
                go_in(h, 2, d).wait_recv()
                go_in_q(h, 2, d).start()

    def cache_near():
        for d in (1, 3):
            along_x(cac, c_s, c_r, d).wait_recv()
            half_x(cac, c_s, c_r, d).start()
            to_sib(cac, c_s, c_r, d).start()

    def cache_far():
        for d in (1, 3):
            half_x(cac, c_s, c_r, d).wait_recv()
        to_sib(cac, c_s, c_r, 2).start()

    def send_slab(h, o):
        n = SLAB[h, o]
        pbf[n] = part[n].astype(BF16)
        far_sends(h, o)

    for d in range(4):
        to_sib(txt, t_s, t_r, d).wait_recv()

    def sib(buf, rec, base, d):
        return rc(buf.at[d], rec.at[d], x_s.at[base + d], x_r.at[base + d], dev(dc=1))

    def xfar(buf, rec, base, d):
        h = pl.ds(d // 2 * HALF, HALF)
        return rc(buf.at[2, h], rec.at[0, h], x_s.at[base + d], x_r.at[base + d], dev(dx=d))

    def xnear(buf, rec, base, d):
        return rc(buf.at[d], rec.at[d], x_s.at[base + 3 + d], x_r.at[base + 3 + d], dev(dx=d))

    def owner_grad(b):
        spots = hot[b]
        both = jnp.concatenate([spots, spots], axis=0)
        return mm(both, sgr[b].reshape(2 * ROWS, D), TN)

    def cache_to_sibling():
        for d in (2, 1, 3, 0):
            csib[d] = owner_grad(2 * d + 1).astype(BF16)
            sib(csib, crec, 4, d).start()

    def cache_far_sends():
        for d in (2, 1, 3, 0):
            cgrad[d] = owner_grad(2 * d)
            sib(csib, crec, 4, d).wait_recv()
            cgrad[d] += crec[d].astype(F32)
            if d == 2:
                csx[2] = cgrad[2].astype(BF16)
                for e in (1, 3):
                    xfar(csx, crx, 16, e).start()

    def cache_near_sends():
        for d in (1, 3):
            xfar(csx, crx, 16, d).wait_recv()
            h = d // 2 * HALF
            csx[d] = cgrad[d].astype(BF16)
            csx[d, h : h + HALF] = (cgrad[d, h : h + HALF] + crx[0, h : h + HALF].astype(F32)).astype(BF16)
            xnear(csx, crx, 16, d).start()

    def cache_result():
        for d in (1, 3):
            xnear(csx, crx, 16, d).wait_recv()
        cg_out[...] = cgrad[0] + crx[1].astype(F32) + crx[3].astype(F32)

    def step(t, carried):
        @pl.when(t == 0)
        def _():
            in_quarters(1, 0)

        @pl.when(t == 1)
        def _():
            edges()
            cache_near()
            in_quarters(1, 1)

        @pl.when(t == 2)
        def _():
            in_quarters(0, 1)

        @pl.when(t == 3)
        def _():
            cache_far()
            in_quarters(1, 3)

        @pl.when(t == 4)
        def _():
            gather_rows()
            mate_step(0, 0)
            mate_step(0, 1)
            send_slab(1, 0)
            mate_step(1, 0)
            mate_step(1, 1)
            send_slab(1, 1)
            mate_step(3, 0)
            in_quarters(0, 0)
            mate_step(2, 0)
            send_slab(0, 1)
            mate_step(3, 1)
            send_slab(1, 3)
            near_sends(1, 0)
            in_quarters(0, 2)
            in_quarters(0, 3)
            in_quarters(1, 2)
            mate_step(2, 1)
            cache_to_sibling()
            near_sends(1, 1)

        text_step(t)
        after = {4: ((0, 1), (1, 3)), 5: ((0, 2),), 6: ((1, 2),), 7: ((0, 3),)}
        for n in range(4, 8):
            @pl.when(t == n)
            def _():
                far_sends(*ORDER[n])
                for key in after[n]:
                    near_sends(*key)
                if n == 4:
                    cache_far_sends()
                if n == 5:
                    cache_near_sends()

        return carried

    lax.fori_loop(0, 8, step, 0)

    for d in (2, 1, 3, 0):
        tsib[d] = tgrad[(2 * d + 1) * ROWS : (2 * d + 2) * ROWS].astype(BF16)
        sib(tsib, trec, 0, d).start()
    sib(tsib, trec, 0, 2).wait_recv()
    tsx[2] = (tgrad[4 * ROWS : 5 * ROWS] + trec[2].astype(F32)).astype(BF16)
    for e in (1, 3):
        xfar(tsx, trx, 8, e).start()
    inner_sum(0, 2)
    near_sends(0, 0)
    inner_sum(1, 2)
    for d in (1, 3):
        h = d // 2 * HALF
        sib(tsib, trec, 0, d).wait_recv()
        share = tgrad[2 * d * ROWS : (2 * d + 1) * ROWS] + trec[d].astype(F32)
        xfar(tsx, trx, 8, d).wait_recv()
        tsx[d] = share.astype(BF16)
        tsx[d, h : h + HALF] = (share[h : h + HALF] + trx[0, h : h + HALF].astype(F32)).astype(BF16)
        xnear(tsx, trx, 8, d).start()
    inner_sum(0, 1)
    outer_send(0, 1)
    inner_sum(1, 1)
    outer_send(1, 1)
    inner_sum(1, 3)
    outer_send(1, 3)
    inner_sum(0, 3)
    outer_send(0, 3)
    inner_sum(1, 0)
    cache_result()
    inner_sum(0, 0)
    for h in (1, 0):
        for d in (1, 3):
            unear(h, d).wait_recv()
        ig_out[h * HALF : h * HALF + HALF] = part[SLAB[h, 0], 0] + uh[h, 1].astype(F32) + uh[h, 3].astype(F32)
    sib(tsib, trec, 0, 0).wait_recv()
    for d in (1, 3):
        xnear(tsx, trx, 8, d).wait_recv()
    tg_out[...] = tgrad[0:ROWS] + trec[0].astype(F32) + trx[1].astype(F32) + trx[3].astype(F32)

    for d in (1, 3):
        for h in (0, 1):
            go_out(h, d).wait_send()
            go_out_q(h, d).wait_send()
            for o in range(4):
                go_in(h, o, d).wait_send()
                go_in_q(h, o, d).wait_send()
                far(h, o, d).wait_send()
                near(h, o, d).wait_send()
            ufar(h, d).wait_send()
            unear(h, d).wait_send()
        for ref, ss, sr in ((txt, t_s, t_r), (cac, c_s, c_r)):
            along_x(ref, ss, sr, d).wait_send()
            half_x(ref, ss, sr, d).wait_send()
        for buf, rec, base in ((tsx, trx, 8), (csx, crx, 16)):
            xfar(buf, rec, base, d).wait_send()
            xnear(buf, rec, base, d).wait_send()
    for dz, dy in plane:
        tbl_to(dz, dy).wait_send()
    for d in range(4):
        to_sib(txt, t_s, t_r, d).wait_send()
        to_sib(cac, c_s, c_r, d).wait_send()
        sib(tsib, trec, 0, d).wait_send()
        sib(csib, crec, 4, d).wait_send()


def place_out(a, b, c, a_out, b_out, c_out, held, sems):
    ways = tuple(enumerate(((a, a_out), (b, b_out), (c, c_out))))
    into = [pltpu.make_async_copy(s, held.at[n], sems.at[n]) for n, (s, _) in ways]
    out = [pltpu.make_async_copy(held.at[n], t, sems.at[3 + n]) for n, (_, t) in ways]
    for copy in into:
        copy.start()
    for first, then in zip(into, out):
        first.wait()
        then.start()
    for copy in out:
        copy.wait()


def shards(images, texts, cache, mate_owner, mate_row, mate_count, log_scale, bias):
    vm = pl.BlockSpec(memory_space=pltpu.VMEM)
    dma = pltpu.SemaphoreType.DMA
    out = jax.ShapeDtypeStruct((ROWS, D), F32)
    four = lambda rows: pltpu.VMEM((4, rows, D), BF16)
    grads = (
        pl.pallas_call(
            kernel,
            out_shape=(out, out, out),
            in_specs=[vm] * 8,
            out_specs=(vm, vm, vm),
            scratch_shapes=[
                pltpu.VMEM((8, 4, HALF, D), BF16),
                pltpu.VMEM((8 * ROWS, D), BF16),
                pltpu.VMEM((8 * ROWS, D), BF16),
                pltpu.VMEM((8, ROWS, D), BF16),
                pltpu.VMEM((4, 4, 16, ROWS), I32),
                pltpu.VMEM((2 * ROWS, 8 * ROWS), BF16),
                pltpu.VMEM((8 * ROWS, D), F32),
                pltpu.VMEM((8, 4, HALF, D), F32),
                pltpu.VMEM((8, 4, HALF, D), BF16),
                pltpu.VMEM((8, 2, ROWS, D), BF16),
                pltpu.VMEM((2, 2, 4, QTR, D), BF16),
                pltpu.VMEM((2, 2, 4, HALF, D), BF16),
                pltpu.VMEM((2, 4, HALF, D), BF16),
                pltpu.VMEM((2, HALF, D), BF16),
                pltpu.VMEM((2, 4, HALF, D), BF16),
                four(ROWS), four(ROWS), four(ROWS), four(ROWS),
                four(ROWS), four(ROWS), four(ROWS), four(ROWS),
                pltpu.VMEM((4, ROWS, D), F32),
                pltpu.VMEM((8, ROWS, ROWS), BF16),
                dma((2, 4, 4)), dma((2, 4, 4)), dma((2, 2, 5)), dma((2, 2, 5)),
                dma((12,)), dma((12,)), dma((12,)), dma((12,)),
                dma((4, 4)), dma((4, 4)),
                dma((2, 2, 4)), dma((2, 2, 4)), dma((2, 2, 4)), dma((2, 2, 4)),
                dma((2, 8)), dma((2, 8)), dma((24,)), dma((24,)),
            ],
            compiler_params=pltpu.CompilerParams(
                collective_id=0, has_side_effects=True, vmem_limit_bytes=62 << 20
            ),
            cost_estimate=pl.CostEstimate(flops=17_000_000_000, bytes_accessed=4_000_000, transcendentals=2_000_000),
        )(
            log_scale.reshape(1, 1), bias.reshape(1, 1), images, texts, cache,
            mate_owner.T, mate_row.T, mate_count.reshape(1, ROWS),
        )
    )
    anywhere = pl.BlockSpec(memory_space=pl.ANY)
    return tuple(
        pl.pallas_call(
            place_out,
            out_shape=(out, out, out),
            in_specs=[anywhere] * 3,
            out_specs=(anywhere,) * 3,
            scratch_shapes=[pltpu.VMEM((3, ROWS, D), F32), dma((6,))],
        )(*grads)
    )


def solution(mesh):
    rows = P(("blk", "img"), None)
    return jax.shard_map(
        shards,
        mesh=mesh,
        in_specs=(rows, rows, rows, rows, rows, P(("blk", "img")), P(), P()),
        out_specs=(rows, rows, rows),
        check_vma=False,
    )
```
